32 devices in a mesh: frame: 8 (over z, x), row: 4 (over y, core).
Axes of the slice: x: 2, y: 2, z: 4, core: 2. Of those that a mesh axis runs over, the one named last changes fastest.
Arguments:
- query_in: bfloat16 [32, 4, 8, 2240], P('frame', 'row'), may hold values from -6 to 6
- key_in: bfloat16 [32, 4, 8, 2240], P('frame', 'row'), may hold values from -24 to 24, as said below
- value_in: bfloat16 [32, 4, 8, 2240], P('frame', 'row'), may hold values from -32 to 32, as said below
- hidden_in: bfloat16 [32, 4, 8, 2240], P('frame', 'row'), may hold values from -16 to 16, as said below
- out_weight: bfloat16 [2240, 2240], replicated, may hold values from -0.125 to 0.125
- norm_gain: float32 [2240], replicated, may hold values from 0.25 to 1.75
- temporal_taps: float32 [3, 2240], replicated, may hold values from -3.5 to 3.5
- block_valid: int32 [8], P('frame'), may hold values from 1 to 4, as said below
Outputs:
- mixed: bfloat16 [32, 4, 8, 2240], P('frame', 'row')
The draws below stay inside these ranges and needn't reach their ends.
Inputs may be any that keep to these rules, and one draw needn't show every extreme that they name: key_in lies within this range. value_in lies within this range. hidden_in lies within this range. `block_valid`: the first frame block is full.
All inputs are finite; a program needn't handle non-finite values.
Results may differ from the reference program's by a relative error of at most 0.0058.
Values may be sent and summed in bfloat16 or wider, within the bound.
A program may use at most 128 MiB of HBM per device.

```python
import math
import jax
import jax.numpy as jnp
from jax import lax

D = 2240
HEADS = 20
DH = 112
FB = 4
KT = 3
F = 32
HR = 4
WC = 8
N_FRAME = 8


def head_order(order_key):
    return jax.random.permutation(order_key, DH)


def tied_fields(key):
    noise_key, scale_key, order_key = jax.random.split(jax.random.fold_in(key, 11), 3)
    blocks = F // FB
    shape_full = (blocks, FB, HR, WC, HEADS, DH)
    raw_field = jnp.clip(jax.random.normal(noise_key, shape_full, jnp.float32), -4.0, 4.0)
    log_scale = jax.random.uniform(scale_key, (blocks, 1, HR, 1, HEADS, 1), jnp.float32, math.log(0.3), math.log(3.0))
    centre = 0.0293
    strength = 8.0
    key_field = jnp.exp(log_scale) * (raw_field - 1.5)
    feature = jnp.maximum(raw_field - 1.5, 0.0) - centre
    orders = jax.vmap(head_order)(jax.random.split(order_key, HEADS))
    head_index = jnp.arange(HEADS)[:, None]
    tied_part = strength * feature[:, :, :, :, head_index, orders]
    return (key_field.reshape(F, HR, WC, D), tied_part.reshape(F, HR, WC, D))


def draw_key_in(key, part):
    key_field, tied_part = tied_fields(key)
    return key_field.astype(jnp.bfloat16)


def draw_value_in(key, part):
    key_field, tied_part = tied_fields(key)
    noise_key, shared_key = jax.random.split(jax.random.fold_in(key, 23), 2)
    blocks = F // FB
    shape_full = (blocks, FB, HR, WC, D)
    shared = jnp.clip(jax.random.normal(shared_key, (blocks, 1, HR, 1, D), jnp.float32), -4.0, 4.0)
    noise_field = jnp.clip(jax.random.normal(noise_key, shape_full, jnp.float32), -4.0, 4.0)
    values_full = noise_field + 1.5 * shared
    return (values_full.reshape(F, HR, WC, D) + tied_part).astype(jnp.bfloat16)


def draw_hidden_in(key, part):
    noise_key, row_key, column_key = jax.random.split(jax.random.fold_in(key, 37), 3)
    row_scale = jnp.exp(jax.random.uniform(row_key, (F, HR, WC, 1), jnp.float32, math.log(0.2), math.log(2.0)))
    column_scale = jnp.exp(jax.random.uniform(column_key, (1, 1, 1, D), jnp.float32, math.log(0.2), math.log(2.0)))
    noise_field = jnp.clip(jax.random.normal(noise_key, (F, HR, WC, D), jnp.float32), -4.0, 4.0)
    field = noise_field * row_scale * column_scale
    return field.astype(jnp.bfloat16)


def draw_block_valid(key, part):
    counts = jax.random.randint(jax.random.fold_in(key, 51), (N_FRAME,), 1, FB + 1)
    return jnp.where(jnp.arange(N_FRAME) == 0, FB, counts).astype(jnp.int32)


def levels(stream_key, dims, cuts, low, top_value):
    level, own = 1.0, jax.random.fold_in(stream_key, 6)
    for dim, blocks in cuts:
        draws = jnp.exp(jax.random.uniform(jax.random.fold_in(own, dim), (blocks,), jnp.float32, low / len(cuts), top_value / len(cuts)))
        level = level * jnp.repeat(draws, dims[dim] // blocks).reshape([-1 if axis == dim else 1 for axis in range(len(dims))])
    return level


def noise(rng, dims, scale, bound, cuts=(), kind=jnp.bfloat16):
    entries = scale * jax.random.normal(rng, dims, jnp.float32)
    if cuts:
        entries = entries * levels(rng, dims, cuts, -0.22, 0.18)
    return jnp.clip(entries, -bound, bound).astype(kind)


def setup_inputs(seed: int = 0) -> dict:
    keys = jax.random.split(jax.random.key(seed), 9)
    return {
        "query_in": noise(keys[0], (F, HR, WC, D), 1.0, 6.0, ((0, 8), (1, 4))),
        "key_in": draw_key_in(jax.random.fold_in(keys[8], 71), 0),
        "value_in": draw_value_in(jax.random.fold_in(keys[8], 71), 0),
        "hidden_in": draw_hidden_in(jax.random.fold_in(keys[8], 71), 0),
        "out_weight": noise(keys[4], (D, D), D ** -0.5, 0.125),
        "norm_gain": jnp.clip(1.0 + 0.15 * jax.random.normal(keys[5], (D,), jnp.float32), 0.25, 1.75),
        "temporal_taps": noise(keys[6], (KT, D), KT ** -0.5, 3.5, (), jnp.float32),
        "block_valid": draw_block_valid(jax.random.fold_in(keys[8], 71), 0),
    }


EPS_DEN = 1e-06
EPS_NORM = 1e-06

def reference(query_in, key_in, value_in, hidden_in, out_weight, norm_gain, temporal_taps, block_valid):
    highest = lax.Precision.HIGHEST
    frame_pos = jnp.tile(jnp.arange(FB, dtype=jnp.int32), N_FRAME)
    frame_limit = jnp.repeat(block_valid, FB)
    frame_mask = (frame_pos < frame_limit).astype(jnp.float32)
    block_mask = frame_mask.reshape(N_FRAME, FB)
    block_ids = jnp.arange(N_FRAME, dtype=jnp.int32)

    def block_state(block_index):
        anchor = (block_index * FB).astype(jnp.int32)
        key_block = lax.dynamic_slice_in_dim(key_in, anchor, FB, 0).astype(jnp.float32)
        value_block = lax.dynamic_slice_in_dim(value_in, anchor, FB, 0).astype(jnp.float32)
        frame_weight = lax.dynamic_index_in_dim(block_mask, block_index, 0, keepdims=False)
        key_feat = (jnp.maximum(key_block, 0.0) * frame_weight[:, None, None, None]).reshape(-1, HEADS, DH)
        value_feat = value_block.reshape(-1, HEADS, DH)
        local_state = jnp.einsum('thi,thj->hij', key_feat, value_feat, precision=highest)
        local_norm = lax.optimization_barrier(jnp.sum(key_feat, axis=0))
        return (local_state, local_norm)
    states, norms = lax.map(block_state, block_ids)
    total_states = jnp.cumsum(states, axis=0).astype(jnp.bfloat16)
    total_norms = jnp.cumsum(norms, axis=0).astype(jnp.bfloat16)

    def block_output(block_index):
        anchor = (block_index * FB).astype(jnp.int32)
        query_block = lax.dynamic_slice_in_dim(query_in, anchor, FB, 0).astype(jnp.float32)
        hidden_block = lax.dynamic_slice_in_dim(hidden_in, anchor, FB, 0)
        frame_weight = lax.dynamic_index_in_dim(block_mask, block_index, 0, keepdims=False)
        state_now = lax.dynamic_index_in_dim(total_states, block_index, 0, keepdims=False).astype(jnp.float32)
        norm_now = lax.dynamic_index_in_dim(total_norms, block_index, 0, keepdims=False).astype(jnp.float32)
        query_feat = jnp.maximum(query_block, 0.0).reshape(-1, HEADS, DH)
        numerator = jnp.einsum('thi,hij->thj', query_feat, state_now, precision=highest)
        denominator = jnp.einsum('thi,hi->th', query_feat, norm_now, precision=highest) + EPS_DEN
        token_mask = jnp.broadcast_to(frame_weight[:, None, None], (FB, HR, WC)).reshape(-1, 1, 1)
        attended = (numerator / denominator[:, :, None] * token_mask).reshape(-1, D).astype(jnp.bfloat16)
        projected = jnp.dot(attended, out_weight, preferred_element_type=jnp.float32)
        residual = (hidden_block.reshape(-1, D).astype(jnp.float32) + projected).astype(jnp.bfloat16)
        residual_f = lax.optimization_barrier(residual).astype(jnp.float32)
        inverse = lax.rsqrt(lax.optimization_barrier(jnp.mean(residual_f * residual_f, axis=-1, keepdims=True)) + EPS_NORM)
        normed = (residual_f * inverse * norm_gain).astype(jnp.bfloat16)
        return (residual.reshape(FB, HR, WC, D), normed.reshape(FB, HR, WC, D))
    residuals, normeds = lax.map(block_output, block_ids)
    residual_all = residuals.reshape(F, HR, WC, D)
    normed_all = normeds.reshape(F, HR, WC, D)
    leading = jnp.zeros((KT - 1, HR, WC, D), jnp.bfloat16)
    extended = jnp.concatenate([leading, normed_all], axis=0)
    temporal = jnp.zeros((F, HR, WC, D), jnp.float32)
    for offset in range(KT):
        lower = KT - 1 - offset
        temporal = temporal + temporal_taps[offset] * extended[lower:lower + F].astype(jnp.float32)
    temporal = temporal.astype(jnp.bfloat16)
    temporal_f = lax.optimization_barrier(temporal).astype(jnp.float32)
    return (residual_all.astype(jnp.float32) + temporal_f).astype(jnp.bfloat16)
```

```python
import functools

import jax
import jax.numpy as jnp
from jax import lax
from jax.experimental import pallas as pl
from jax.experimental.pallas import tpu as pltpu
from jax.sharding import PartitionSpec as P

HEADS = 20
EPS_DEN = 1e-06
EPS_NORM = 1e-06
LANES = 128
TILE = 256


def kernel(
    n_frame, n_row, group, slots,
    q_hbm, k_hbm, v_hbm, h_hbm, w_hbm, gain_ref, taps_ref, valid_ref,
    out_ref,
    q_in, k_in, v_in, h_in, w_in, kv_out, kv_all, q_out, q_all, state_in, state_out,
    att_out, att_all, att, res, ext,
    in_sem, w_sem, kv_send, kv_recv, q_send, q_recv, s_send, s_recv, a_send, a_recv, halo_sem,
):
    frames, rows_dev, cols, feats = q_in.shape
    tokens = frames * rows_dev * cols
    per_frame = rows_dev * cols
    dh = feats // HEADS
    peers = group * n_row
    planes = n_frame // group
    taps_n = taps_ref.shape[0]
    halo = (taps_n - 1) * per_frame
    bf16, f32 = jnp.bfloat16, jnp.float32

    f, r = lax.axis_index("frame"), lax.axis_index("row")
    plane, inner = f // group, f % group
    me = inner * n_row + r

    def place(rank):
        return {"frame": plane * group + rank // n_row, "row": rank % n_row}

    def at_frame(index):
        return {"frame": index, "row": r}

    def others(step):
        return (me + step) % peers

    loads = [
        pltpu.make_async_copy(src, dst, in_sem.at[i])
        for i, (src, dst) in enumerate(((k_hbm, k_in), (v_hbm, v_in), (q_hbm, q_in), (h_hbm, h_in)))
    ]
    for load in loads:
        load.start()
    barrier = pltpu.get_barrier_semaphore()

    def greet(device):
        pl.semaphore_signal(barrier, inc=1, device_id=device, device_id_type=pl.DeviceIdType.MESH)

    for step in range(1, peers):
        greet(place(others(step)))
    partners = ((f >= group, f - group), (f < n_frame - group, f + group))
    if group > 1:
        partners += (((inner == 0) & (f > 0), f - 1), ((inner == group - 1) & (f < n_frame - 1), f + 1))
    for there, index in partners:
        pl.when(there)(functools.partial(greet, at_frame(index)))

    w_loads = [
        pltpu.make_async_copy(
            w_hbm.at[pl.ds(h * dh, dh), :], w_in.at[h, pl.ds(0, dh), :], w_sem.at[h]
        )
        for h in range(HEADS)
    ]
    for load in w_loads:
        load.start()

    token_frame = lax.broadcasted_iota(jnp.int32, (tokens, 1), 0) // per_frame
    mask = token_frame < valid_ref[0]

    def put(dst, first, value, tail):
        for h in range(peers * slots):
            if h < HEADS:
                full = jnp.concatenate([value[:, h * dh : (h + 1) * dh], tail], axis=1)
            else:
                full = jnp.zeros((tokens, LANES), bf16)
            lane = (h % slots) * LANES
            dst[h // slots, first : first + tokens, lane : lane + LANES] = full

    zeros = jnp.zeros((tokens, LANES - dh), bf16)
    ones = (lax.broadcasted_iota(jnp.int32, (tokens, LANES - dh), 1) == 0).astype(f32).astype(bf16)

    loads[0].wait()
    key = k_in[...].astype(f32).reshape(tokens, feats)
    put(kv_out, 0, jnp.where(mask, jnp.maximum(key, 0.0), 0.0).astype(bf16), zeros)
    loads[1].wait()
    put(kv_out, tokens, v_in[...].astype(f32).reshape(tokens, feats).astype(bf16), ones)

    pl.semaphore_wait(barrier, peers - 1 + sum(there.astype(jnp.int32) for there, _ in partners))

    def exchange(out, all_, send, recv):
        copies = [
            pltpu.make_async_remote_copy(
                src_ref=out.at[others(step)],
                dst_ref=all_.at[me],
                send_sem=send.at[step],
                recv_sem=recv.at[step],
                device_id=place(others(step)),
                device_id_type=pl.DeviceIdType.MESH,
            )
            for step in range(1, peers)
        ]
        for copy in copies:
            copy.start()
        all_[pl.ds(me, 1)] = out[pl.ds(me, 1)]
        return copies

    kv_copies = exchange(kv_out, kv_all, kv_send, kv_recv)

    loads[2].wait()
    query = q_in[...].astype(f32).reshape(tokens, feats)
    put(q_out, 0, jnp.where(mask, jnp.maximum(query, 0.0), 0.0).astype(bf16), zeros)
    q_copies = exchange(q_out, q_all, q_send, q_recv)

    w_in[:, dh:, :] = jnp.zeros((HEADS, LANES - dh, feats), bf16)

    for copy in kv_copies:
        copy.wait_recv()

    block_states = []
    for s in range(slots):
        lane = slice(s * LANES, (s + 1) * LANES)
        mine = []
        for g in range(group):
            ranks = slice(g * n_row, (g + 1) * n_row)
            keys = kv_all[ranks, 0:tokens, lane].reshape(n_row * tokens, LANES)
            values = kv_all[ranks, tokens : 2 * tokens, lane].reshape(n_row * tokens, LANES)
            mine.append(
                lax.dot_general(
                    keys, values, (((0,), (0,)), ((), ())), preferred_element_type=f32
                )[:dh]
            )
        block_states.append(mine)

    def pass_on(s):
        return pltpu.make_async_remote_copy(
            src_ref=state_out.at[s],
            dst_ref=state_in.at[s],
            send_sem=s_send.at[s],
            recv_sem=s_recv.at[s],
            device_id=at_frame(f + group),
            device_id_type=pl.DeviceIdType.MESH,
        )

    @pl.when(plane == 0)
    def _():
        state_in[...] = jnp.zeros(state_in.shape, bf16)

    totals = []
    for s in range(slots):
        pl.when(plane > 0)(lambda s=s: pass_on(s).wait_recv())
        running = state_in[s].astype(f32)
        mine = []
        for g in range(group):
            running = running + block_states[s][g]
            mine.append(running.astype(bf16))
        totals.append(mine)
        state_out[s] = mine[-1]
        pl.when(plane < planes - 1)(lambda s=s: pass_on(s).start())

    for copy in q_copies:
        copy.wait_recv()
    for s in range(slots):
        lane = slice(s * LANES, (s + 1) * LANES)
        for g in range(group):
            ranks = slice(g * n_row, (g + 1) * n_row)
            queries = q_all[ranks, :, lane].reshape(n_row * tokens, LANES)[:, :dh]
            both = jnp.dot(queries, totals[s][g], preferred_element_type=f32)
            value = both / (both[:, dh : dh + 1] + EPS_DEN)
            att_out[ranks, :, lane] = value.astype(bf16).reshape(n_row, tokens, LANES)
    a_copies = exchange(att_out, att_all, a_send, a_recv)

    loads[3].wait()
    for load in w_loads:
        load.wait()
    for copy in a_copies:
        copy.wait_recv()
    depth = HEADS * LANES
    for p in range(peers):
        low = p * slots * LANES
        width = min(slots * LANES, depth - low)
        if width > 0:
            att[:, low : low + width] = att_all[p, :, 0:width]

    def project(start, width):
        weights = w_in[:, :, pl.ds(start, width)].reshape(depth, width)
        projected = jnp.dot(att[...], weights, preferred_element_type=f32)
        hidden = h_in[:, :, :, pl.ds(start, width)].astype(f32).reshape(tokens, width)
        residual = (hidden + projected).astype(bf16).astype(f32)
        res[:, pl.ds(start, width)] = residual
        return jnp.sum(residual * residual, axis=1, keepdims=True)

    whole = feats // TILE

    def tile(i, total):
        return total + project(pl.multiple_of(i * TILE, TILE), TILE)

    square = lax.fori_loop(0, whole, tile, jnp.zeros((tokens, 1), f32))
    if feats % TILE:
        square = square + project(whole * TILE, feats % TILE)
    inverse = lax.rsqrt(square / feats + EPS_NORM)
    gain = gain_ref[...].reshape(1, feats)
    ext[halo:, :] = (res[...] * inverse * gain).astype(bf16)

    to_next = pltpu.make_async_remote_copy(
        src_ref=ext.at[pl.ds(tokens, halo), :],
        dst_ref=ext.at[pl.ds(0, halo), :],
        send_sem=halo_sem.at[0],
        recv_sem=halo_sem.at[1],
        device_id=at_frame(f + 1),
        device_id_type=pl.DeviceIdType.MESH,
    )
    pl.when(f < n_frame - 1)(lambda: to_next.start())

    @pl.when(f == 0)
    def _():
        ext[0:halo, :] = jnp.zeros((halo, feats), bf16)

    pl.when(f > 0)(lambda: to_next.wait_recv())
    normed = ext[...].astype(f32)
    taps = taps_ref[...]
    temporal = jnp.zeros((tokens, feats), f32)
    for j in range(taps_n):
        low = (taps_n - 1 - j) * per_frame
        temporal = temporal + taps[j : j + 1] * normed[low : low + tokens]
    mixed = res[...] + temporal.astype(bf16).astype(f32)
    out_ref[...] = mixed.reshape(out_ref.shape).astype(bf16)

    for copy in kv_copies + q_copies + a_copies:
        copy.wait_send()

    @pl.when(plane < planes - 1)
    def _():
        for s in range(slots):
            pass_on(s).wait_send()

    pl.when(f < n_frame - 1)(lambda: to_next.wait_send())


def body(n_frame, n_row, query_in, key_in, value_in, hidden_in, out_weight, norm_gain, temporal_taps, block_valid):
    frames, rows_dev, cols, feats = query_in.shape
    tokens = frames * rows_dev * cols
    group = 2 if n_frame % 2 == 0 else 1
    peers = group * n_row
    slots = -(-HEADS // peers)
    dh = feats // HEADS
    halo = (temporal_taps.shape[0] - 1) * rows_dev * cols
    width = slots * LANES
    bf16 = jnp.bfloat16
    any_ = pl.BlockSpec(memory_space=pl.ANY)
    vmem = pl.BlockSpec(memory_space=pltpu.VMEM)
    smem = pl.BlockSpec(memory_space=pltpu.SMEM)
    sems = pltpu.SemaphoreType.DMA
    return pl.pallas_call(
        functools.partial(kernel, n_frame, n_row, group, slots),
        out_shape=jax.ShapeDtypeStruct(query_in.shape, bf16),
        in_specs=[any_] * 5 + [vmem, vmem, smem],
        out_specs=vmem,
        scratch_shapes=[
            pltpu.VMEM(query_in.shape, bf16),
            pltpu.VMEM(query_in.shape, bf16),
            pltpu.VMEM(query_in.shape, bf16),
            pltpu.VMEM(query_in.shape, bf16),
            pltpu.VMEM((HEADS, LANES, feats), bf16),
            pltpu.VMEM((peers, 2 * tokens, width), bf16),
            pltpu.VMEM((peers, 2 * tokens, width), bf16),
            pltpu.VMEM((peers, tokens, width), bf16),
            pltpu.VMEM((peers, tokens, width), bf16),
            pltpu.VMEM((slots, dh, LANES), bf16),
            pltpu.VMEM((slots, dh, LANES), bf16),
            pltpu.VMEM((peers, tokens, width), bf16),
            pltpu.VMEM((peers, tokens, width), bf16),
            pltpu.VMEM((tokens, HEADS * LANES), bf16),
            pltpu.VMEM((tokens, feats), jnp.float32),
            pltpu.VMEM((tokens + halo, feats), bf16),
            sems((4,)),
            sems((HEADS,)),
            sems((peers,)),
            sems((peers,)),
            sems((peers,)),
            sems((peers,)),
            sems((slots,)),
            sems((slots,)),
            sems((peers,)),
            sems((peers,)),
            sems((2,)),
        ],
        compiler_params=pltpu.CompilerParams(
            collective_id=0, has_side_effects=True, vmem_limit_bytes=52 * 1024 * 1024
        ),
        cost_estimate=pl.CostEstimate(
            flops=2 * tokens * feats * feats, bytes_accessed=2 * feats * feats, transcendentals=0
        ),
        name="block_forward",
    )(query_in, key_in, value_in, hidden_in, out_weight, norm_gain, temporal_taps, block_valid)


def solution(mesh):
    split = P("frame", "row", None, None)
    placed = (split, split, split, split, P(), P(), P(), P("frame"))
    n_frame, n_row = mesh.shape["frame"], mesh.shape["row"]
    return jax.shard_map(
        functools.partial(body, n_frame, n_row),
        mesh=mesh,
        in_specs=placed,
        out_specs=split,
        check_vma=False,
    )
```

```python
import functools

import jax
import jax.numpy as jnp
from jax import lax
from jax.experimental import pallas as pl
from jax.experimental.pallas import tpu as pltpu
from jax.sharding import PartitionSpec as P

HEADS = 20
EPS_DEN = 1e-06
EPS_NORM = 1e-06
LANES = 128


def kernel(
    n_frame, n_row, group, slots,
    q_hbm, k_hbm, v_hbm, h_hbm, w_hbm, gain_hbm, taps_hbm, valid_ref,
    out_ref,
    q_in, k_in, v_in, h_in, gain_in, taps_in, w_in, kv_out, kv_all, q_out, q_all,
    state, total, state_in, state_out, att_out, att_all, res, ext,
    in_sem, w_sem, kv_send, kv_recv, q_send, q_recv, s_send, s_recv, a_send, a_recv, halo_sem,
):
    frames, rows_dev, cols, feats = q_in.shape
    tokens = frames * rows_dev * cols
    per_frame = rows_dev * cols
    dh = feats // HEADS
    peers = group * n_row
    planes = n_frame // group
    taps_n = taps_in.shape[0]
    halo = (taps_n - 1) * per_frame
    bf16, f32 = jnp.bfloat16, jnp.float32

    f, r = lax.axis_index("frame"), lax.axis_index("row")
    plane, inner = f // group, f % group
    me = inner * n_row + r

    def place(rank):
        return {"frame": plane * group + rank // n_row, "row": rank % n_row}

    def at_frame(index):
        return {"frame": index, "row": r}

    def others(step):
        return (me + step) % peers

    def first(rank):
        return (rank * HEADS + peers - 1) // peers

    def owned(rank):
        return first(rank + 1) - first(rank)

    def where_owned(rank, s, act):
        if s < HEADS // peers:
            act()
        else:
            pl.when(owned(rank) > s)(act)

    def owners(s):
        return [p for p in range(peers) if owned(p) > s]

    loads = [
        pltpu.make_async_copy(src, dst, in_sem.at[i])
        for i, (src, dst) in enumerate(
            (
                (k_hbm, k_in), (v_hbm, v_in), (q_hbm, q_in), (h_hbm, h_in),
                (gain_hbm, gain_in), (taps_hbm, taps_in),
            )
        )
    ]
    for load in loads:
        load.start()
    barrier = pltpu.get_barrier_semaphore()

    def greet(device):
        pl.semaphore_signal(barrier, inc=1, device_id=device, device_id_type=pl.DeviceIdType.MESH)

    for step in range(1, peers):
        greet(place(others(step)))
    partners = ((f >= group, f - group), (f < n_frame - group, f + group))
    if group > 1:
        partners += (((inner == 0) & (f > 0), f - 1), ((inner == group - 1) & (f < n_frame - 1), f + 1))
    for there, index in partners:
        pl.when(there)(functools.partial(greet, at_frame(index)))

    w_loads = []
    w_first = [0]
    for s in range(slots):
        for p in owners(s):
            i = len(w_loads)
            w_loads.append(
                pltpu.make_async_copy(
                    w_hbm.at[pl.ds((first(p) + s) * dh, dh), :], w_in.at[i, pl.ds(0, dh), :], w_sem.at[i]
                )
            )
        w_first.append(len(w_loads))

    token_frame = lax.broadcasted_iota(jnp.int32, (tokens, 1), 0) // per_frame
    mask = token_frame < valid_ref[0]
    zeros = jnp.zeros((tokens, LANES - dh), bf16)
    ones = (lax.broadcasted_iota(jnp.int32, (tokens, LANES - dh), 1) == 0).astype(f32).astype(bf16)

    def put(dst, s, low, value, tail):
        for p in owners(s):
            h = first(p) + s
            dst[s, p, low : low + tokens] = jnp.concatenate([value[:, h * dh : (h + 1) * dh], tail], axis=1)

    def feature(ref):
        return jnp.where(mask, jnp.maximum(ref[...].astype(f32).reshape(tokens, feats), 0.0), 0.0).astype(bf16)

    class Exchange:
        def __init__(self, out, all_, send, recv):
            self.refs = out, all_, send, recv

        def copy(self, s, step):
            out, all_, send, recv = self.refs
            return pltpu.make_async_remote_copy(
                src_ref=out.at[s, others(step)],
                dst_ref=all_.at[s, me],
                send_sem=send.at[s, step],
                recv_sem=recv.at[s, step],
                device_id=place(others(step)),
                device_id_type=pl.DeviceIdType.MESH,
            )

        def start(self, s):
            out, all_, _, _ = self.refs
            for step in range(1, peers):
                where_owned(others(step), s, lambda step=step: self.copy(s, step).start())

            def keep():
                all_[s, pl.ds(me, 1)] = out[s, pl.ds(me, 1)]

            where_owned(me, s, keep)

        def arrived(self, s):
            for step in range(1, peers):
                self.copy(s, step).wait_recv()

        def sent(self, s):
            for step in range(1, peers):
                where_owned(others(step), s, lambda step=step: self.copy(s, step).wait_send())

    kv = Exchange(kv_out, kv_all, kv_send, kv_recv)
    query = Exchange(q_out, q_all, q_send, q_recv)

    loads[0].wait()
    key_feat = feature(k_in)
    loads[1].wait()
    value_feat = v_in[...].astype(f32).reshape(tokens, feats).astype(bf16)
    for s in range(slots):
        put(kv_out, s, 0, key_feat, zeros)
        put(kv_out, s, tokens, value_feat, ones)
        if s == 0:
            pl.semaphore_wait(barrier, peers - 1 + sum(there.astype(jnp.int32) for there, _ in partners))
        kv.start(s)
    for load in w_loads:
        load.start()
    loads[2].wait()
    query_feat = feature(q_in)
    for s in range(slots):
        put(q_out, s, 0, query_feat, zeros)
        query.start(s)
    w_in[:, dh:, :] = jnp.zeros((HEADS, LANES - dh, feats), bf16)

    def pass_on(s):
        return pltpu.make_async_remote_copy(
            src_ref=state_out.at[s],
            dst_ref=state_in.at[s],
            send_sem=s_send.at[s],
            recv_sem=s_recv.at[s],
            device_id=at_frame(f + group),
            device_id_type=pl.DeviceIdType.MESH,
        )

    def ranks(g):
        return slice(g * n_row, (g + 1) * n_row)

    def plane_state(s):
        kv.arrived(s)
        mine = []
        for g in range(group):
            keys = kv_all[s, ranks(g), 0:tokens].reshape(n_row * tokens, LANES)
            values = kv_all[s, ranks(g), tokens : 2 * tokens].reshape(n_row * tokens, LANES)
            mine.append(
                lax.dot_general(
                    keys, values, (((0,), (0,)), ((), ())), preferred_element_type=f32
                )[:dh]
            )
            state[s, g] = mine[-1]

        @pl.when(plane == 0)
        def _():
            state_in[s] = jnp.zeros((dh, LANES), bf16)
            state_out[s] = sum(mine[1:], mine[0]).astype(bf16)
            if planes > 1:
                pass_on(s).start()

    def chain(s):
        pl.when(plane > 0)(lambda: pass_on(s).wait_recv())
        running = state_in[s].astype(f32)
        for g in range(group):
            running = running + state[s, g]
            total[s, g] = running.astype(bf16)

        @pl.when((plane > 0) & (plane < planes - 1))
        def _():
            state_out[s] = running.astype(bf16)
            pass_on(s).start()

    back = Exchange(att_out, att_all, a_send, a_recv)

    def attend(s):
        query.arrived(s)
        for g in range(group):
            queries = q_all[s, ranks(g)].reshape(n_row * tokens, LANES)[:, :dh]
            both = jnp.dot(queries, total[s, g], preferred_element_type=f32)
            value = both / (both[:, dh : dh + 1] + EPS_DEN)
            att_out[s, ranks(g)] = value.astype(bf16).reshape(n_row, tokens, LANES)

    def give_back(s):
        def mine():
            attend(s)
            for step in range(1, peers):
                back_copy(s, step).start()
            att_all[s, pl.ds(me, 1)] = att_out[s, pl.ds(me, 1)]

        where_owned(me, s, mine)

    def back_copy(s, step):
        return back.copy(s, step)

    stages = [(s + lag, lag, s) for s in range(slots) for lag in range(3)]
    for _, lag, s in sorted(stages):
        if lag == 0:
            where_owned(me, s, lambda s=s: plane_state(s))
        elif lag == 1:
            where_owned(me, s, lambda s=s: chain(s))
        else:
            give_back(s)

    loads[3].wait()
    half = -(-feats // (2 * LANES)) * LANES
    square = jnp.zeros((tokens, 1), f32)
    for s in range(slots):
        here = owners(s)
        for load in w_loads[w_first[s] : w_first[s + 1]]:
            load.wait()
        for step in range(1, peers):
            where_owned((me + peers - step) % peers, s, lambda step=step: back_copy(s, step).wait_recv())
        att = jnp.concatenate([att_all[s, p] for p in here], axis=1)
        depth = len(here) * LANES
        for low, high in ((0, half), (half, feats)):
            weights = w_in[w_first[s] : w_first[s + 1], :, low:high].reshape(depth, high - low)
            summed = jnp.dot(att, weights, preferred_element_type=f32)
            if s > 0:
                summed = res[:, low:high] + summed
            if s == slots - 1:
                hidden = h_in[:, :, :, low:high].astype(f32).reshape(tokens, high - low)
                summed = (hidden + summed).astype(bf16).astype(f32)
                square = square + jnp.sum(summed * summed, axis=1, keepdims=True)
            res[:, low:high] = summed
    inverse = lax.rsqrt(square / feats + EPS_NORM)
    loads[4].wait()
    gain = gain_in[...].reshape(1, feats)
    ext[halo:, :] = (res[...] * inverse * gain).astype(bf16)

    to_next = pltpu.make_async_remote_copy(
        src_ref=ext.at[pl.ds(tokens, halo), :],
        dst_ref=ext.at[pl.ds(0, halo), :],
        send_sem=halo_sem.at[0],
        recv_sem=halo_sem.at[1],
        device_id=at_frame(f + 1),
        device_id_type=pl.DeviceIdType.MESH,
    )
    pl.when(f < n_frame - 1)(lambda: to_next.start())

    @pl.when(f == 0)
    def _():
        ext[0:halo, :] = jnp.zeros((halo, feats), bf16)

    for s in range(slots):
        kv.sent(s)
        query.sent(s)

        def gone(s=s):
            for step in range(1, peers):
                back_copy(s, step).wait_send()
            pl.when(plane < planes - 1)(lambda: pass_on(s).wait_send())

        where_owned(me, s, gone)
    loads[5].wait()
    pl.when(f > 0)(lambda: to_next.wait_recv())
    normed = ext[...].astype(f32)
    taps = taps_in[...]
    temporal = jnp.zeros((tokens, feats), f32)
    for j in range(taps_n):
        low = (taps_n - 1 - j) * per_frame
        temporal = temporal + taps[j : j + 1] * normed[low : low + tokens]
    mixed = res[...] + temporal.astype(bf16).astype(f32)
    out_ref[...] = mixed.reshape(out_ref.shape).astype(bf16)
    pl.when(f < n_frame - 1)(lambda: to_next.wait_send())


def body(n_frame, n_row, query_in, key_in, value_in, hidden_in, out_weight, norm_gain, temporal_taps, block_valid):
    frames, rows_dev, cols, feats = query_in.shape
    tokens = frames * rows_dev * cols
    group = 2 if n_frame % 2 == 0 else 1
    peers = group * n_row
    slots = -(-HEADS // peers)
    dh = feats // HEADS
    halo = (temporal_taps.shape[0] - 1) * rows_dev * cols
    bf16, f32 = jnp.bfloat16, jnp.float32
    hbm = pl.BlockSpec(memory_space=pltpu.HBM)
    vmem = pl.BlockSpec(memory_space=pltpu.VMEM)
    smem = pl.BlockSpec(memory_space=pltpu.SMEM)
    sems = pltpu.SemaphoreType.DMA
    return pl.pallas_call(
        functools.partial(kernel, n_frame, n_row, group, slots),
        out_shape=jax.ShapeDtypeStruct(query_in.shape, bf16),
        in_specs=[hbm] * 7 + [smem],
        out_specs=vmem,
        scratch_shapes=[
            pltpu.VMEM(query_in.shape, bf16),
            pltpu.VMEM(query_in.shape, bf16),
            pltpu.VMEM(query_in.shape, bf16),
            pltpu.VMEM(query_in.shape, bf16),
            pltpu.VMEM(norm_gain.shape, f32),
            pltpu.VMEM(temporal_taps.shape, f32),
            pltpu.VMEM((HEADS, LANES, feats), bf16),
            pltpu.VMEM((slots, peers, 2 * tokens, LANES), bf16),
            pltpu.VMEM((slots, peers, 2 * tokens, LANES), bf16),
            pltpu.VMEM((slots, peers, tokens, LANES), bf16),
            pltpu.VMEM((slots, peers, tokens, LANES), bf16),
            pltpu.VMEM((slots, group, dh, LANES), f32),
            pltpu.VMEM((slots, group, dh, LANES), bf16),
            pltpu.VMEM((slots, dh, LANES), bf16),
            pltpu.VMEM((slots, dh, LANES), bf16),
            pltpu.VMEM((slots, peers, tokens, LANES), bf16),
            pltpu.VMEM((slots, peers, tokens, LANES), bf16),
            pltpu.VMEM((tokens, feats), f32),
            pltpu.VMEM((tokens + halo, feats), bf16),
            sems((6,)),
            sems((HEADS,)),
            sems((slots, peers)),
            sems((slots, peers)),
            sems((slots, peers)),
            sems((slots, peers)),
            sems((slots,)),
            sems((slots,)),
            sems((slots, peers)),
            sems((slots, peers)),
            sems((2,)),
        ],
        compiler_params=pltpu.CompilerParams(
            collective_id=0, has_side_effects=True, vmem_limit_bytes=63 * 1024 * 1024
        ),
        cost_estimate=pl.CostEstimate(
            flops=2 * tokens * feats * feats, bytes_accessed=2 * feats * feats, transcendentals=0
        ),
        name="block_forward",
    )(query_in, key_in, value_in, hidden_in, out_weight, norm_gain, temporal_taps, block_valid)


def solution(mesh):
    split = P("frame", "row", None, None)
    placed = (split, split, split, split, P(), P(), P(), P("frame"))
    n_frame, n_row = mesh.shape["frame"], mesh.shape["row"]
    return jax.shard_map(
        functools.partial(body, n_frame, n_row),
        mesh=mesh,
        in_specs=placed,
        out_specs=split,
        check_vma=False,
    )
```

```python
import functools

import jax
import jax.numpy as jnp
from jax import lax
from jax.experimental import pallas as pl
from jax.experimental.pallas import tpu as pltpu
from jax.sharding import PartitionSpec as P

HEADS = 20
EPS_DEN = 1e-06
EPS_NORM = 1e-06
LANES = 128


def kernel(
    n_frame, n_row, group, slots,
    q_hbm, k_hbm, v_hbm, h_hbm, w_hbm, gain_hbm, taps_hbm, valid_ref,
    out_ref,
    q_in, k_in, v_in, h_in, gain_in, taps_in, w_in, kv_out, kv_all, q_out, q_all,
    state, total, state_in, state_out, att_out, att_all, res, ext,
    in_sem, w_sem, kv_send, kv_recv, q_send, q_recv, s_send, s_recv, a_send, a_recv, halo_sem,
):
    frames, rows_dev, cols, feats = q_in.shape
    tokens = frames * rows_dev * cols
    per_frame = rows_dev * cols
    dh = feats // HEADS
    peers = group * n_row
    planes = n_frame // group
    taps_n = taps_in.shape[0]
    halo = (taps_n - 1) * per_frame
    bf16, f32 = jnp.bfloat16, jnp.float32

    f, r = lax.axis_index("frame"), lax.axis_index("row")
    plane, inner = f // group, f % group
    me = inner * n_row + r

    def place(rank):
        return {"frame": plane * group + rank // n_row, "row": rank % n_row}

    def at_frame(index):
        return {"frame": index, "row": r}

    def others(step):
        return (me + step) % peers

    def first(rank):
        return (rank * HEADS + peers - 1) // peers

    def owned(rank):
        return first(rank + 1) - first(rank)

    def where_owned(rank, s, act):
        if s < HEADS // peers:
            act()
        else:
            pl.when(owned(rank) > s)(act)

    def owners(s):
        return [p for p in range(peers) if owned(p) > s]

    loads = [
        pltpu.make_async_copy(src, dst, in_sem.at[i])
        for i, (src, dst) in enumerate(
            (
                (k_hbm, k_in), (v_hbm, v_in), (q_hbm, q_in), (h_hbm, h_in),
                (gain_hbm, gain_in), (taps_hbm, taps_in),
            )
        )
    ]
    for load in loads:
        load.start()
    barrier = pltpu.get_barrier_semaphore()

    def greet(device):
        pl.semaphore_signal(barrier, inc=1, device_id=device, device_id_type=pl.DeviceIdType.MESH)

    for step in range(1, peers):
        greet(place(others(step)))
    for step in range(1, planes):
        greet(at_frame((f + step * group) % n_frame))
    partners = ()
    if group > 1:
        partners = (((inner == 0) & (f > 0), f - 1), ((inner == group - 1) & (f < n_frame - 1), f + 1))
    for there, index in partners:
        pl.when(there)(functools.partial(greet, at_frame(index)))

    w_loads = []
    w_first = [0]
    for s in range(slots):
        for p in owners(s):
            i = len(w_loads)
            w_loads.append(
                pltpu.make_async_copy(
                    w_hbm.at[pl.ds((first(p) + s) * dh, dh), :], w_in.at[i, pl.ds(0, dh), :], w_sem.at[i]
                )
            )
        w_first.append(len(w_loads))

    token_frame = lax.broadcasted_iota(jnp.int32, (tokens, 1), 0) // per_frame
    mask = token_frame < valid_ref[0]
    zeros = jnp.zeros((tokens, LANES - dh), bf16)
    ones = (lax.broadcasted_iota(jnp.int32, (tokens, LANES - dh), 1) == 0).astype(f32).astype(bf16)

    def put(dst, s, low, value, tail):
        for p in owners(s):
            h = first(p) + s
            dst[s, p, low : low + tokens] = jnp.concatenate([value[:, h * dh : (h + 1) * dh], tail], axis=1)

    def feature(ref):
        return jnp.where(mask, jnp.maximum(ref[...].astype(f32).reshape(tokens, feats), 0.0), 0.0).astype(bf16)

    class Exchange:
        def __init__(self, out, all_, send, recv):
            self.refs = out, all_, send, recv

        def copy(self, s, step):
            out, all_, send, recv = self.refs
            return pltpu.make_async_remote_copy(
                src_ref=out.at[s, others(step)],
                dst_ref=all_.at[s, me],
                send_sem=send.at[s, step],
                recv_sem=recv.at[s, step],
                device_id=place(others(step)),
                device_id_type=pl.DeviceIdType.MESH,
            )

        def start(self, s):
            out, all_, _, _ = self.refs
            for step in range(1, peers):
                where_owned(others(step), s, lambda step=step: self.copy(s, step).start())

            def keep():
                all_[s, pl.ds(me, 1)] = out[s, pl.ds(me, 1)]

            where_owned(me, s, keep)

        def arrived(self, s):
            for step in range(1, peers):
                self.copy(s, step).wait_recv()

        def sent(self, s):
            for step in range(1, peers):
                where_owned(others(step), s, lambda step=step: self.copy(s, step).wait_send())

    kv = Exchange(kv_out, kv_all, kv_send, kv_recv)
    query = Exchange(q_out, q_all, q_send, q_recv)

    loads[0].wait()
    key_feat = feature(k_in)
    loads[1].wait()
    value_feat = v_in[...].astype(f32).reshape(tokens, feats).astype(bf16)
    for s in range(slots):
        put(kv_out, s, 0, key_feat, zeros)
        put(kv_out, s, tokens, value_feat, ones)
        if s == 0:
            near = sum(there.astype(jnp.int32) for there, _ in partners)
            pl.semaphore_wait(barrier, peers - 1 + planes - 1 + near)
        if s < 2:
            kv.start(s)
    for load in w_loads:
        load.start()
    loads[2].wait()
    query_feat = feature(q_in)
    for s in range(slots):
        put(q_out, s, 0, query_feat, zeros)
    w_in[:, dh:, :] = jnp.zeros((HEADS, LANES - dh, feats), bf16)
    queue = [functools.partial(kv.start, s) for s in range(2, slots)]
    queue += [functools.partial(query.start, s) for s in range(slots)]

    rounds = range((planes - 1).bit_length())

    def pass_on(s, l, k):
        return pltpu.make_async_remote_copy(
            src_ref=state_out.at[s],
            dst_ref=state_in.at[s, l],
            send_sem=s_send.at[s, k],
            recv_sem=s_recv.at[s, l],
            device_id=at_frame(f + (1 + k) * group),
            device_id_type=pl.DeviceIdType.MESH,
        )

    def sender(l):
        return (plane + 1) % 2 ** (l + 1) == 2**l

    def receiver(l):
        return (plane // 2**l) % 2 == 1

    def each_target(s, l, act):
        for k in range(2**l):
            pl.when(sender(l) & (plane + 1 + k < planes))(lambda k=k: act(pass_on(s, l, k)))

    def send_state(s, l, value):
        @pl.when(sender(l))
        def _():
            state_out[s] = value.astype(bf16)

        each_target(s, l, lambda copy: copy.start())

    def ranks(g):
        return slice(g * n_row, (g + 1) * n_row)

    def plane_state(s):
        kv.arrived(s)
        mine = []
        for g in range(group):
            keys = kv_all[s, ranks(g), 0:tokens].reshape(n_row * tokens, LANES)
            values = kv_all[s, ranks(g), tokens : 2 * tokens].reshape(n_row * tokens, LANES)
            mine.append(
                lax.dot_general(
                    keys, values, (((0,), (0,)), ((), ())), preferred_element_type=f32
                )[:dh]
            )
            state[s, g] = mine[-1]

        send_state(s, 0, sum(mine[1:], mine[0]))

    def chain(s):
        running = jnp.zeros((dh, LANES), f32)
        here = [state[s, g] for g in range(group)]
        for l in rounds:
            if l > 0:
                send_state(s, l, sum(here, running))

            @pl.when(receiver(l))
            def _():
                pass_on(s, l, 0).wait_recv()

            @pl.when(jnp.logical_not(receiver(l)))
            def _():
                state_in[s, l] = jnp.zeros((dh, LANES), bf16)

            running = running + state_in[s, l].astype(f32)
        for g in range(group):
            running = running + here[g]
            total[s, g] = running.astype(bf16)

    back = Exchange(att_out, att_all, a_send, a_recv)

    def attend(s):
        query.arrived(s)
        for g in range(group):
            queries = q_all[s, ranks(g)].reshape(n_row * tokens, LANES)[:, :dh]
            both = jnp.dot(queries, total[s, g], preferred_element_type=f32)
            value = both / (both[:, dh : dh + 1] + EPS_DEN)
            att_out[s, ranks(g)] = value.astype(bf16).reshape(n_row, tokens, LANES)

    def give_back(s):
        def mine():
            attend(s)
            for step in range(1, peers):
                back_copy(s, step).start()
            att_all[s, pl.ds(me, 1)] = att_out[s, pl.ds(me, 1)]

        where_owned(me, s, mine)

    def back_copy(s, step):
        return back.copy(s, step)

    stages = [(s + lag, lag, s) for s in range(slots) for lag in range(3)]
    for _, lag, s in sorted(stages):
        if lag == 0:
            where_owned(me, s, lambda s=s: plane_state(s))
            for start in queue[s : s + 1] if s < slots - 1 else queue[s:]:
                start()
        elif lag == 1:
            where_owned(me, s, lambda s=s: chain(s))
        else:
            give_back(s)

    loads[3].wait()
    half = -(-feats // (2 * LANES)) * LANES
    square = jnp.zeros((tokens, 1), f32)
    for s in range(slots):
        here = owners(s)
        for load in w_loads[w_first[s] : w_first[s + 1]]:
            load.wait()
        for step in range(1, peers):
            where_owned((me + peers - step) % peers, s, lambda step=step: back_copy(s, step).wait_recv())
        att = jnp.concatenate([att_all[s, p] for p in here], axis=1)
        depth = len(here) * LANES
        for low, high in ((0, half), (half, feats)):
            weights = w_in[w_first[s] : w_first[s + 1], :, low:high].reshape(depth, high - low)
            summed = jnp.dot(att, weights, preferred_element_type=f32)
            if s > 0:
                summed = res[:, low:high] + summed
            if s == slots - 1:
                hidden = h_in[:, :, :, low:high].astype(f32).reshape(tokens, high - low)
                summed = (hidden + summed).astype(bf16).astype(f32)
                square = square + jnp.sum(summed * summed, axis=1, keepdims=True)
            res[:, low:high] = summed
    inverse = lax.rsqrt(square / feats + EPS_NORM)
    loads[4].wait()
    gain = gain_in[...].reshape(1, feats)
    ext[halo:, :] = (res[...] * inverse * gain).astype(bf16)

    to_next = pltpu.make_async_remote_copy(
        src_ref=ext.at[pl.ds(tokens, halo), :],
        dst_ref=ext.at[pl.ds(0, halo), :],
        send_sem=halo_sem.at[0],
        recv_sem=halo_sem.at[1],
        device_id=at_frame(f + 1),
        device_id_type=pl.DeviceIdType.MESH,
    )
    pl.when(f < n_frame - 1)(lambda: to_next.start())

    @pl.when(f == 0)
    def _():
        ext[0:halo, :] = jnp.zeros((halo, feats), bf16)

    for s in range(slots):
        kv.sent(s)
        query.sent(s)

        def gone(s=s):
            for step in range(1, peers):
                back_copy(s, step).wait_send()
            for l in rounds:
                each_target(s, l, lambda copy: copy.wait_send())

        where_owned(me, s, gone)
    loads[5].wait()
    pl.when(f > 0)(lambda: to_next.wait_recv())
    normed = ext[...].astype(f32)
    taps = taps_in[...]
    temporal = jnp.zeros((tokens, feats), f32)
    for j in range(taps_n):
        low = (taps_n - 1 - j) * per_frame
        temporal = temporal + taps[j : j + 1] * normed[low : low + tokens]
    mixed = res[...] + temporal.astype(bf16).astype(f32)
    out_ref[...] = mixed.reshape(out_ref.shape).astype(bf16)
    pl.when(f < n_frame - 1)(lambda: to_next.wait_send())


def body(n_frame, n_row, query_in, key_in, value_in, hidden_in, out_weight, norm_gain, temporal_taps, block_valid):
    frames, rows_dev, cols, feats = query_in.shape
    tokens = frames * rows_dev * cols
    group = 2 if n_frame % 2 == 0 else 1
    peers = group * n_row
    slots = -(-HEADS // peers)
    planes = n_frame // group
    rounds = max((planes - 1).bit_length(), 1)
    dh = feats // HEADS
    halo = (temporal_taps.shape[0] - 1) * rows_dev * cols
    bf16, f32 = jnp.bfloat16, jnp.float32
    hbm = pl.BlockSpec(memory_space=pltpu.HBM)
    vmem = pl.BlockSpec(memory_space=pltpu.VMEM)
    smem = pl.BlockSpec(memory_space=pltpu.SMEM)
    sems = pltpu.SemaphoreType.DMA
    return pl.pallas_call(
        functools.partial(kernel, n_frame, n_row, group, slots),
        out_shape=jax.ShapeDtypeStruct(query_in.shape, bf16),
        in_specs=[hbm] * 7 + [smem],
        out_specs=vmem,
        scratch_shapes=[
            pltpu.VMEM(query_in.shape, bf16),
            pltpu.VMEM(query_in.shape, bf16),
            pltpu.VMEM(query_in.shape, bf16),
            pltpu.VMEM(query_in.shape, bf16),
            pltpu.VMEM(norm_gain.shape, f32),
            pltpu.VMEM(temporal_taps.shape, f32),
            pltpu.VMEM((HEADS, LANES, feats), bf16),
            pltpu.VMEM((slots, peers, 2 * tokens, LANES), bf16),
            pltpu.VMEM((slots, peers, 2 * tokens, LANES), bf16),
            pltpu.VMEM((slots, peers, tokens, LANES), bf16),
            pltpu.VMEM((slots, peers, tokens, LANES), bf16),
            pltpu.VMEM((slots, group, dh, LANES), f32),
            pltpu.VMEM((slots, group, dh, LANES), bf16),
            pltpu.VMEM((slots, rounds, dh, LANES), bf16),
            pltpu.VMEM((slots, dh, LANES), bf16),
            pltpu.VMEM((slots, peers, tokens, LANES), bf16),
            pltpu.VMEM((slots, peers, tokens, LANES), bf16),
            pltpu.VMEM((tokens, feats), f32),
            pltpu.VMEM((tokens + halo, feats), bf16),
            sems((6,)),
            sems((HEADS,)),
            sems((slots, peers)),
            sems((slots, peers)),
            sems((slots, peers)),
            sems((slots, peers)),
            sems((slots, max(planes // 2, 1))),
            sems((slots, rounds)),
            sems((slots, peers)),
            sems((slots, peers)),
            sems((2,)),
        ],
        compiler_params=pltpu.CompilerParams(
            collective_id=0, has_side_effects=True, vmem_limit_bytes=63 * 1024 * 1024
        ),
        cost_estimate=pl.CostEstimate(
            flops=2 * tokens * feats * feats, bytes_accessed=2 * feats * feats, transcendentals=0
        ),
        name="block_forward",
    )(query_in, key_in, value_in, hidden_in, out_weight, norm_gain, temporal_taps, block_valid)


def solution(mesh):
    split = P("frame", "row", None, None)
    placed = (split, split, split, split, P(), P(), P(), P("frame"))
    n_frame, n_row = mesh.shape["frame"], mesh.shape["row"]
    return jax.shard_map(
        functools.partial(body, n_frame, n_row),
        mesh=mesh,
        in_specs=placed,
        out_specs=split,
        check_vma=False,
    )
```

```python
import functools

import jax
import jax.numpy as jnp
from jax import lax
from jax.experimental import pallas as pl
from jax.experimental.pallas import tpu as pltpu
from jax.sharding import PartitionSpec as P

HEADS = 20
EPS_DEN = 1e-06
EPS_NORM = 1e-06
LANES = 128


def kernel(
    n_frame, n_row, group, slots,
    q_hbm, k_hbm, v_hbm, h_hbm, w_hbm, gain_hbm, taps_hbm, valid_ref,
    out_ref,
    q_in, k_in, v_in, h_in, gain_in, taps_in, w_in, kv_out, kv_all, q_out, q_all,
    state, total, state_in, state_out, att_out, att_all, res, ext,
    in_sem, w_sem, kv_send, kv_recv, q_send, q_recv, s_send, s_recv, a_send, a_recv, halo_sem,
):
    frames, rows_dev, cols, feats = q_in.shape
    tokens = frames * rows_dev * cols
    per_frame = rows_dev * cols
    dh = feats // HEADS
    peers = group * n_row
    planes = n_frame // group
    taps_n = taps_in.shape[0]
    halo = (taps_n - 1) * per_frame
    bf16, f32 = jnp.bfloat16, jnp.float32

    f, r = lax.axis_index("frame"), lax.axis_index("row")
    plane, inner = f // group, f % group
    me = inner * n_row + r

    def place(rank):
        return {"frame": plane * group + rank // n_row, "row": rank % n_row}

    def at_frame(index):
        return {"frame": index, "row": r}

    def others(step):
        return (me + step) % peers

    def first(rank):
        return (rank * HEADS + peers - 1) // peers

    def owned(rank):
        return first(rank + 1) - first(rank)

    def where_owned(rank, s, act):
        if s < HEADS // peers:
            act()
        else:
            pl.when(owned(rank) > s)(act)

    def owners(s):
        return [p for p in range(peers) if owned(p) > s]

    loads = [
        pltpu.make_async_copy(src, dst, in_sem.at[i])
        for i, (src, dst) in enumerate(
            (
                (k_hbm, k_in), (v_hbm, v_in), (q_hbm, q_in), (h_hbm, h_in),
                (gain_hbm, gain_in), (taps_hbm, taps_in),
            )
        )
    ]
    for load in loads:
        load.start()
    barrier = pltpu.get_barrier_semaphore()

    def greet(device):
        pl.semaphore_signal(barrier, inc=1, device_id=device, device_id_type=pl.DeviceIdType.MESH)

    for step in range(1, peers):
        greet(place(others(step)))
    for step in range(1, planes):
        greet(at_frame((f + step * group) % n_frame))
    partners = ()
    if group > 1:
        partners = (((inner == 0) & (f > 0), f - 1), ((inner == group - 1) & (f < n_frame - 1), f + 1))
    for there, index in partners:
        pl.when(there)(functools.partial(greet, at_frame(index)))

    w_loads = []
    w_first = [0]
    for s in range(slots):
        for p in owners(s):
            i = len(w_loads)
            w_loads.append(
                pltpu.make_async_copy(
                    w_hbm.at[pl.ds((first(p) + s) * dh, dh), :], w_in.at[i, pl.ds(0, dh), :], w_sem.at[i]
                )
            )
        w_first.append(len(w_loads))

    token_frame = lax.broadcasted_iota(jnp.int32, (tokens, 1), 0) // per_frame
    mask = token_frame < valid_ref[0]
    zeros = jnp.zeros((tokens, LANES - dh), bf16)
    ones = (lax.broadcasted_iota(jnp.int32, (tokens, LANES - dh), 1) == 0).astype(f32).astype(bf16)

    def put(dst, s, low, value, tail):
        for p in owners(s):
            h = first(p) + s
            dst[s, p, low : low + tokens] = jnp.concatenate([value[:, h * dh : (h + 1) * dh], tail], axis=1)

    def feature(ref):
        return jnp.where(mask, jnp.maximum(ref[...].astype(f32).reshape(tokens, feats), 0.0), 0.0).astype(bf16)

    class Exchange:
        def __init__(self, out, all_, send, recv):
            self.refs = out, all_, send, recv

        def copy(self, s, step):
            out, all_, send, recv = self.refs
            return pltpu.make_async_remote_copy(
                src_ref=out.at[s, others(step)],
                dst_ref=all_.at[s, me],
                send_sem=send.at[s, step],
                recv_sem=recv.at[s, step],
                device_id=place(others(step)),
                device_id_type=pl.DeviceIdType.MESH,
            )

        def start(self, s):
            out, all_, _, _ = self.refs
            for step in range(1, peers):
                where_owned(others(step), s, lambda step=step: self.copy(s, step).start())

            def keep():
                all_[s, pl.ds(me, 1)] = out[s, pl.ds(me, 1)]

            where_owned(me, s, keep)

        def arrived(self, s):
            for step in range(1, peers):
                self.copy(s, step).wait_recv()

        def sent(self, s):
            for step in range(1, peers):
                where_owned(others(step), s, lambda step=step: self.copy(s, step).wait_send())

    kv = Exchange(kv_out, kv_all, kv_send, kv_recv)
    query = Exchange(q_out, q_all, q_send, q_recv)

    loads[0].wait()
    key_feat = feature(k_in)
    loads[1].wait()
    value_feat = v_in[...].astype(f32).reshape(tokens, feats).astype(bf16)
    for s in range(slots):
        put(kv_out, s, 0, key_feat, zeros)
        put(kv_out, s, tokens, value_feat, ones)
        if s == 0:
            near = sum(there.astype(jnp.int32) for there, _ in partners)
            pl.semaphore_wait(barrier, peers - 1 + planes - 1 + near)
        kv.start(s)
    for load in w_loads:
        load.start()
    loads[2].wait()
    query_feat = feature(q_in)
    for s in range(slots):
        put(q_out, s, 0, query_feat, zeros)
        query.start(s)
    w_in[:, dh:, :] = jnp.zeros((HEADS, LANES - dh, feats), bf16)
    rounds = range((planes - 1).bit_length())

    def pass_on(s, l, k):
        return pltpu.make_async_remote_copy(
            src_ref=state_out.at[s],
            dst_ref=state_in.at[s, l],
            send_sem=s_send.at[s, k],
            recv_sem=s_recv.at[s, l],
            device_id=at_frame(f + (1 + k) * group),
            device_id_type=pl.DeviceIdType.MESH,
        )

    def sender(l):
        return (plane + 1) % 2 ** (l + 1) == 2**l

    def receiver(l):
        return (plane // 2**l) % 2 == 1

    def each_target(s, l, act):
        for k in range(2**l):
            pl.when(sender(l) & (plane + 1 + k < planes))(lambda k=k: act(pass_on(s, l, k)))

    def send_state(s, l, value):
        @pl.when(sender(l))
        def _():
            state_out[s] = value.astype(bf16)

        each_target(s, l, lambda copy: copy.start())

    def ranks(g):
        return slice(g * n_row, (g + 1) * n_row)

    def plane_state(s):
        kv.arrived(s)
        mine = []
        for g in range(group):
            keys = kv_all[s, ranks(g), 0:tokens].reshape(n_row * tokens, LANES)
            values = kv_all[s, ranks(g), tokens : 2 * tokens].reshape(n_row * tokens, LANES)
            mine.append(
                lax.dot_general(
                    keys, values, (((0,), (0,)), ((), ())), preferred_element_type=f32
                )[:dh]
            )
            state[s, g] = mine[-1]

        send_state(s, 0, sum(mine[1:], mine[0]))

    def chain(s):
        running = jnp.zeros((dh, LANES), f32)
        here = [state[s, g] for g in range(group)]
        for l in rounds:
            if l > 0:
                send_state(s, l, sum(here, running))

            @pl.when(receiver(l))
            def _():
                pass_on(s, l, 0).wait_recv()

            @pl.when(jnp.logical_not(receiver(l)))
            def _():
                state_in[s, l] = jnp.zeros((dh, LANES), bf16)

            running = running + state_in[s, l].astype(f32)
        for g in range(group):
            running = running + here[g]
            total[s, g] = running.astype(bf16)

    back = Exchange(att_out, att_all, a_send, a_recv)

    def attend(s):
        query.arrived(s)
        for g in range(group):
            queries = q_all[s, ranks(g)].reshape(n_row * tokens, LANES)[:, :dh]
            both = jnp.dot(queries, total[s, g], preferred_element_type=f32)
            value = both / (both[:, dh : dh + 1] + EPS_DEN)
            att_out[s, ranks(g)] = value.astype(bf16).reshape(n_row, tokens, LANES)

    def give_back(s):
        def mine():
            attend(s)
            for step in range(1, peers):
                back_copy(s, step).start()
            att_all[s, pl.ds(me, 1)] = att_out[s, pl.ds(me, 1)]

        where_owned(me, s, mine)

    def back_copy(s, step):
        return back.copy(s, step)

    stages = [(s + lag, lag, s) for s in range(slots) for lag in range(3)]
    for _, lag, s in sorted(stages):
        if lag == 0:
            where_owned(me, s, lambda s=s: plane_state(s))
        elif lag == 1:
            where_owned(me, s, lambda s=s: chain(s))
        else:
            give_back(s)

    loads[3].wait()
    half = -(-feats // (2 * LANES)) * LANES
    square = jnp.zeros((tokens, 1), f32)
    for s in range(slots):
        here = owners(s)
        for load in w_loads[w_first[s] : w_first[s + 1]]:
            load.wait()
        for step in range(1, peers):
            where_owned((me + peers - step) % peers, s, lambda step=step: back_copy(s, step).wait_recv())
        att = jnp.concatenate([att_all[s, p] for p in here], axis=1)
        depth = len(here) * LANES
        for low, high in ((0, half), (half, feats)):
            weights = w_in[w_first[s] : w_first[s + 1], :, low:high].reshape(depth, high - low)
            summed = jnp.dot(att, weights, preferred_element_type=f32)
            if s > 0:
                summed = res[:, low:high] + summed
            if s == slots - 1:
                hidden = h_in[:, :, :, low:high].astype(f32).reshape(tokens, high - low)
                summed = (hidden + summed).astype(bf16).astype(f32)
                square = square + jnp.sum(summed * summed, axis=1, keepdims=True)
            res[:, low:high] = summed
    inverse = lax.rsqrt(square / feats + EPS_NORM)
    loads[4].wait()
    gain = gain_in[...].reshape(1, feats)
    ext[halo:, :] = (res[...] * inverse * gain).astype(bf16)

    to_next = pltpu.make_async_remote_copy(
        src_ref=ext.at[pl.ds(tokens, halo), :],
        dst_ref=ext.at[pl.ds(0, halo), :],
        send_sem=halo_sem.at[0],
        recv_sem=halo_sem.at[1],
        device_id=at_frame(f + 1),
        device_id_type=pl.DeviceIdType.MESH,
    )
    pl.when(f < n_frame - 1)(lambda: to_next.start())

    @pl.when(f == 0)
    def _():
        ext[0:halo, :] = jnp.zeros((halo, feats), bf16)

    for s in range(slots):
        kv.sent(s)
        query.sent(s)

        def gone(s=s):
            for step in range(1, peers):
                back_copy(s, step).wait_send()
            for l in rounds:
                each_target(s, l, lambda copy: copy.wait_send())

        where_owned(me, s, gone)
    loads[5].wait()
    pl.when(f > 0)(lambda: to_next.wait_recv())
    normed = ext[...].astype(f32)
    taps = taps_in[...]
    temporal = jnp.zeros((tokens, feats), f32)
    for j in range(taps_n):
        low = (taps_n - 1 - j) * per_frame
        temporal = temporal + taps[j : j + 1] * normed[low : low + tokens]
    mixed = res[...] + temporal.astype(bf16).astype(f32)
    out_ref[...] = mixed.reshape(out_ref.shape).astype(bf16)
    pl.when(f < n_frame - 1)(lambda: to_next.wait_send())


def body(n_frame, n_row, query_in, key_in, value_in, hidden_in, out_weight, norm_gain, temporal_taps, block_valid):
    frames, rows_dev, cols, feats = query_in.shape
    tokens = frames * rows_dev * cols
    group = 2 if n_frame % 2 == 0 else 1
    peers = group * n_row
    slots = -(-HEADS // peers)
    planes = n_frame // group
    rounds = max((planes - 1).bit_length(), 1)
    dh = feats // HEADS
    halo = (temporal_taps.shape[0] - 1) * rows_dev * cols
    bf16, f32 = jnp.bfloat16, jnp.float32
    hbm = pl.BlockSpec(memory_space=pltpu.HBM)
    vmem = pl.BlockSpec(memory_space=pltpu.VMEM)
    smem = pl.BlockSpec(memory_space=pltpu.SMEM)
    sems = pltpu.SemaphoreType.DMA
    return pl.pallas_call(
        functools.partial(kernel, n_frame, n_row, group, slots),
        out_shape=jax.ShapeDtypeStruct(query_in.shape, bf16),
        in_specs=[hbm] * 7 + [smem],
        out_specs=vmem,
        scratch_shapes=[
            pltpu.VMEM(query_in.shape, bf16),
            pltpu.VMEM(query_in.shape, bf16),
            pltpu.VMEM(query_in.shape, bf16),
            pltpu.VMEM(query_in.shape, bf16),
            pltpu.VMEM(norm_gain.shape, f32),
            pltpu.VMEM(temporal_taps.shape, f32),
            pltpu.VMEM((HEADS, LANES, feats), bf16),
            pltpu.VMEM((slots, peers, 2 * tokens, LANES), bf16),
            pltpu.VMEM((slots, peers, 2 * tokens, LANES), bf16),
            pltpu.VMEM((slots, peers, tokens, LANES), bf16),
            pltpu.VMEM((slots, peers, tokens, LANES), bf16),
            pltpu.VMEM((slots, group, dh, LANES), f32),
            pltpu.VMEM((slots, group, dh, LANES), bf16),
            pltpu.VMEM((slots, rounds, dh, LANES), bf16),
            pltpu.VMEM((slots, dh, LANES), bf16),
            pltpu.VMEM((slots, peers, tokens, LANES), bf16),
            pltpu.VMEM((slots, peers, tokens, LANES), bf16),
            pltpu.VMEM((tokens, feats), f32),
            pltpu.VMEM((tokens + halo, feats), bf16),
            sems((6,)),
            sems((HEADS,)),
            sems((slots, peers)),
            sems((slots, peers)),
            sems((slots, peers)),
            sems((slots, peers)),
            sems((slots, max(planes // 2, 1))),
            sems((slots, rounds)),
            sems((slots, peers)),
            sems((slots, peers)),
            sems((2,)),
        ],
        compiler_params=pltpu.CompilerParams(
            collective_id=0, has_side_effects=True, vmem_limit_bytes=63 * 1024 * 1024
        ),
        cost_estimate=pl.CostEstimate(
            flops=2 * tokens * feats * feats, bytes_accessed=2 * feats * feats, transcendentals=0
        ),
        name="block_forward",
    )(query_in, key_in, value_in, hidden_in, out_weight, norm_gain, temporal_taps, block_valid)


def solution(mesh):
    split = P("frame", "row", None, None)
    placed = (split, split, split, split, P(), P(), P(), P("frame"))
    n_frame, n_row = mesh.shape["frame"], mesh.shape["row"]
    return jax.shard_map(
        functools.partial(body, n_frame, n_row),
        mesh=mesh,
        in_specs=placed,
        out_specs=split,
        check_vma=False,
    )
```

```python
import functools

import jax
import jax.numpy as jnp
from jax import lax
from jax.experimental import pallas as pl
from jax.experimental.pallas import tpu as pltpu
from jax.sharding import PartitionSpec as P

HEADS = 20
EPS_DEN = 1e-06
EPS_NORM = 1e-06
LANES = 128


def kernel(
    n_frame, n_row, group, slots,
    q_hbm, k_hbm, v_hbm, h_hbm, w_hbm, gain_hbm, taps_hbm, valid_ref,
    out_ref,
    q_in, k_in, v_in, h_in, gain_in, taps_in, w_in, kv_out, kv_all, q_out, q_all,
    state, total, state_in, state_out, att_out, att_all, res, ext,
    in_sem, w_sem, kv_send, kv_recv, q_send, q_recv, s_send, s_recv, a_send, a_recv, halo_sem,
):
    frames, rows_dev, cols, feats = q_in.shape
    tokens = frames * rows_dev * cols
    per_frame = rows_dev * cols
    dh = feats // HEADS
    peers = group * n_row
    planes = n_frame // group
    taps_n = taps_in.shape[0]
    halo = (taps_n - 1) * per_frame
    bf16, f32 = jnp.bfloat16, jnp.float32

    f, r = lax.axis_index("frame"), lax.axis_index("row")
    plane, inner = f // group, f % group
    me = inner * n_row + r

    def place(rank):
        return {"frame": plane * group + rank // n_row, "row": rank % n_row}

    def at_frame(index):
        return {"frame": index, "row": r}

    def others(step):
        return (me + step) % peers

    def first(rank):
        return (rank * HEADS + peers - 1) // peers

    def owned(rank):
        return first(rank + 1) - first(rank)

    def where_owned(rank, s, act):
        if s < HEADS // peers:
            act()
        else:
            pl.when(owned(rank) > s)(act)

    def owners(s):
        return [p for p in range(peers) if owned(p) > s]

    loads = [
        pltpu.make_async_copy(src, dst, in_sem.at[i])
        for i, (src, dst) in enumerate(
            (
                (k_hbm, k_in), (v_hbm, v_in), (q_hbm, q_in), (h_hbm, h_in),
                (gain_hbm, gain_in), (taps_hbm, taps_in),
            )
        )
    ]
    for load in loads[:3]:
        load.start()
    barrier = pltpu.get_barrier_semaphore()

    def greet(device):
        pl.semaphore_signal(barrier, inc=1, device_id=device, device_id_type=pl.DeviceIdType.MESH)

    for step in range(1, peers):
        greet(place(others(step)))
    rounds = range((planes - 1).bit_length())

    def sender(l):
        return (plane + 1) % 2 ** (l + 1) == 2**l

    def receiver(l):
        return (plane // 2**l) % 2 == 1

    partners = ()
    for l in rounds:
        partners += tuple((sender(l) & (plane + 1 + k < planes), f + (1 + k) * group) for k in range(2**l))
        partners += ((receiver(l), (plane // 2**l * 2**l - 1) * group + inner),)
    if group > 1:
        partners += (((inner == 0) & (f > 0), f - 1), ((inner == group - 1) & (f < n_frame - 1), f + 1))
    for there, index in partners:
        pl.when(there)(functools.partial(greet, at_frame(index)))

    w_loads = []
    w_first = [0]
    for s in range(slots):
        for p in owners(s):
            i = len(w_loads)
            w_loads.append(
                pltpu.make_async_copy(
                    w_hbm.at[pl.ds((first(p) + s) * dh, dh), :], w_in.at[i, pl.ds(0, dh), :], w_sem.at[i]
                )
            )
        w_first.append(len(w_loads))

    token_frame = lax.broadcasted_iota(jnp.int32, (tokens, 1), 0) // per_frame
    mask = token_frame < valid_ref[0]
    zeros = jnp.zeros((tokens, LANES - dh), bf16)
    ones = (lax.broadcasted_iota(jnp.int32, (tokens, LANES - dh), 1) == 0).astype(f32).astype(bf16)

    def put(dst, s, low, value, tail):
        for p in owners(s):
            h = first(p) + s
            dst[s, p, low : low + tokens] = jnp.concatenate([value[:, h * dh : (h + 1) * dh], tail], axis=1)

    def feature(ref):
        return jnp.where(mask, jnp.maximum(ref[...].astype(f32).reshape(tokens, feats), 0.0), 0.0).astype(bf16)

    class Exchange:
        def __init__(self, out, all_, send, recv):
            self.refs = out, all_, send, recv

        def copy(self, s, step):
            out, all_, send, recv = self.refs
            return pltpu.make_async_remote_copy(
                src_ref=out.at[s, others(step)],
                dst_ref=all_.at[s, me],
                send_sem=send.at[s, step],
                recv_sem=recv.at[s, step],
                device_id=place(others(step)),
                device_id_type=pl.DeviceIdType.MESH,
            )

        def start(self, s):
            out, all_, _, _ = self.refs
            for step in range(1, peers):
                where_owned(others(step), s, lambda step=step: self.copy(s, step).start())

            def keep():
                all_[s, pl.ds(me, 1)] = out[s, pl.ds(me, 1)]

            where_owned(me, s, keep)

        def arrived(self, s):
            for step in range(1, peers):
                self.copy(s, step).wait_recv()

        def sent(self, s):
            for step in range(1, peers):
                where_owned(others(step), s, lambda step=step: self.copy(s, step).wait_send())

    kv = Exchange(kv_out, kv_all, kv_send, kv_recv)
    query = Exchange(q_out, q_all, q_send, q_recv)

    loads[0].wait()
    key_feat = feature(k_in)
    loads[1].wait()
    value_feat = v_in[...].astype(f32).reshape(tokens, feats).astype(bf16)
    for s in range(slots):
        put(kv_out, s, 0, key_feat, zeros)
        put(kv_out, s, tokens, value_feat, ones)
        if s == 0:
            near = sum(there.astype(jnp.int32) for there, _ in partners)
            pl.semaphore_wait(barrier, peers - 1 + near)
        kv.start(s)
    loads[2].wait()
    query_feat = feature(q_in)
    for s in range(slots):
        put(q_out, s, 0, query_feat, zeros)
        query.start(s)
    for load in w_loads + loads[3:]:
        load.start()
    w_in[:, dh:, :] = jnp.zeros((HEADS, LANES - dh, feats), bf16)
    def pass_on(s, l, k):
        return pltpu.make_async_remote_copy(
            src_ref=state_out.at[s],
            dst_ref=state_in.at[s, l],
            send_sem=s_send.at[s, k],
            recv_sem=s_recv.at[s, l],
            device_id=at_frame(f + (1 + k) * group),
            device_id_type=pl.DeviceIdType.MESH,
        )

    def each_target(s, l, act):
        for k in range(2**l):
            pl.when(sender(l) & (plane + 1 + k < planes))(lambda k=k: act(pass_on(s, l, k)))

    def send_state(s, l, value):
        @pl.when(sender(l))
        def _():
            state_out[s] = value.astype(bf16)

        each_target(s, l, lambda copy: copy.start())

    def ranks(g):
        return slice(g * n_row, (g + 1) * n_row)

    def plane_state(s):
        kv.arrived(s)
        mine = []
        for g in range(group):
            keys = kv_all[s, ranks(g), 0:tokens].reshape(n_row * tokens, LANES)
            values = kv_all[s, ranks(g), tokens : 2 * tokens].reshape(n_row * tokens, LANES)
            mine.append(
                lax.dot_general(
                    keys, values, (((0,), (0,)), ((), ())), preferred_element_type=f32
                )[:dh]
            )
            state[s, g] = mine[-1]

        send_state(s, 0, sum(mine[1:], mine[0]))

    def chain(s):
        running = jnp.zeros((dh, LANES), f32)
        here = [state[s, g] for g in range(group)]
        for l in rounds:
            if l > 0:
                send_state(s, l, sum(here, running))

            @pl.when(receiver(l))
            def _():
                pass_on(s, l, 0).wait_recv()

            @pl.when(jnp.logical_not(receiver(l)))
            def _():
                state_in[s, l] = jnp.zeros((dh, LANES), bf16)

            running = running + state_in[s, l].astype(f32)
        for g in range(group):
            running = running + here[g]
            total[s, g] = running.astype(bf16)

    back = Exchange(att_out, att_all, a_send, a_recv)

    def attend(s):
        query.arrived(s)
        for g in range(group):
            queries = q_all[s, ranks(g)].reshape(n_row * tokens, LANES)[:, :dh]
            both = jnp.dot(queries, total[s, g], preferred_element_type=f32)
            value = both / (both[:, dh : dh + 1] + EPS_DEN)
            att_out[s, ranks(g)] = value.astype(bf16).reshape(n_row, tokens, LANES)

    def give_back(s):
        def mine():
            attend(s)
            for step in range(1, peers):
                back_copy(s, step).start()
            att_all[s, pl.ds(me, 1)] = att_out[s, pl.ds(me, 1)]

        where_owned(me, s, mine)

    def back_copy(s, step):
        return back.copy(s, step)

    stages = [(s + lag, lag, s) for s in range(slots) for lag in range(3)]
    for _, lag, s in sorted(stages):
        if lag == 0:
            where_owned(me, s, lambda s=s: plane_state(s))
        elif lag == 1:
            where_owned(me, s, lambda s=s: chain(s))
        else:
            give_back(s)

    loads[3].wait()
    half = -(-feats // (2 * LANES)) * LANES
    square = jnp.zeros((tokens, 1), f32)
    for s in range(slots):
        here = owners(s)
        for load in w_loads[w_first[s] : w_first[s + 1]]:
            load.wait()
        for step in range(1, peers):
            where_owned((me + peers - step) % peers, s, lambda step=step: back_copy(s, step).wait_recv())
        att = jnp.concatenate([att_all[s, p] for p in here], axis=1)
        depth = len(here) * LANES
        for low, high in ((0, half), (half, feats)):
            weights = w_in[w_first[s] : w_first[s + 1], :, low:high].reshape(depth, high - low)
            summed = jnp.dot(att, weights, preferred_element_type=f32)
            if s > 0:
                summed = res[:, low:high] + summed
            if s == slots - 1:
                hidden = h_in[:, :, :, low:high].astype(f32).reshape(tokens, high - low)
                summed = (hidden + summed).astype(bf16).astype(f32)
                square = square + jnp.sum(summed * summed, axis=1, keepdims=True)
            res[:, low:high] = summed
    inverse = lax.rsqrt(square / feats + EPS_NORM)
    loads[4].wait()
    gain = gain_in[...].reshape(1, feats)
    ext[halo:, :] = (res[...] * inverse * gain).astype(bf16)

    to_next = pltpu.make_async_remote_copy(
        src_ref=ext.at[pl.ds(tokens, halo), :],
        dst_ref=ext.at[pl.ds(0, halo), :],
        send_sem=halo_sem.at[0],
        recv_sem=halo_sem.at[1],
        device_id=at_frame(f + 1),
        device_id_type=pl.DeviceIdType.MESH,
    )
    pl.when(f < n_frame - 1)(lambda: to_next.start())

    @pl.when(f == 0)
    def _():
        ext[0:halo, :] = jnp.zeros((halo, feats), bf16)

    for s in range(slots):
        kv.sent(s)
        query.sent(s)

        def gone(s=s):
            for step in range(1, peers):
                back_copy(s, step).wait_send()
            for l in rounds:
                each_target(s, l, lambda copy: copy.wait_send())

        where_owned(me, s, gone)
    loads[5].wait()
    pl.when(f > 0)(lambda: to_next.wait_recv())
    normed = ext[...].astype(f32)
    taps = taps_in[...]
    temporal = jnp.zeros((tokens, feats), f32)
    for j in range(taps_n):
        low = (taps_n - 1 - j) * per_frame
        temporal = temporal + taps[j : j + 1] * normed[low : low + tokens]
    mixed = res[...] + temporal.astype(bf16).astype(f32)
    out_ref[...] = mixed.reshape(out_ref.shape).astype(bf16)
    pl.when(f < n_frame - 1)(lambda: to_next.wait_send())


def body(n_frame, n_row, query_in, key_in, value_in, hidden_in, out_weight, norm_gain, temporal_taps, block_valid):
    frames, rows_dev, cols, feats = query_in.shape
    tokens = frames * rows_dev * cols
    group = 2 if n_frame % 2 == 0 else 1
    peers = group * n_row
    slots = -(-HEADS // peers)
    planes = n_frame // group
    rounds = max((planes - 1).bit_length(), 1)
    dh = feats // HEADS
    halo = (temporal_taps.shape[0] - 1) * rows_dev * cols
    bf16, f32 = jnp.bfloat16, jnp.float32
    hbm = pl.BlockSpec(memory_space=pltpu.HBM)
    vmem = pl.BlockSpec(memory_space=pltpu.VMEM)
    smem = pl.BlockSpec(memory_space=pltpu.SMEM)
    sems = pltpu.SemaphoreType.DMA
    return pl.pallas_call(
        functools.partial(kernel, n_frame, n_row, group, slots),
        out_shape=jax.ShapeDtypeStruct(query_in.shape, bf16),
        in_specs=[hbm] * 7 + [smem],
        out_specs=vmem,
        scratch_shapes=[
            pltpu.VMEM(query_in.shape, bf16),
            pltpu.VMEM(query_in.shape, bf16),
            pltpu.VMEM(query_in.shape, bf16),
            pltpu.VMEM(query_in.shape, bf16),
            pltpu.VMEM(norm_gain.shape, f32),
            pltpu.VMEM(temporal_taps.shape, f32),
            pltpu.VMEM((HEADS, LANES, feats), bf16),
            pltpu.VMEM((slots, peers, 2 * tokens, LANES), bf16),
            pltpu.VMEM((slots, peers, 2 * tokens, LANES), bf16),
            pltpu.VMEM((slots, peers, tokens, LANES), bf16),
            pltpu.VMEM((slots, peers, tokens, LANES), bf16),
            pltpu.VMEM((slots, group, dh, LANES), f32),
            pltpu.VMEM((slots, group, dh, LANES), bf16),
            pltpu.VMEM((slots, rounds, dh, LANES), bf16),
            pltpu.VMEM((slots, dh, LANES), bf16),
            pltpu.VMEM((slots, peers, tokens, LANES), bf16),
            pltpu.VMEM((slots, peers, tokens, LANES), bf16),
            pltpu.VMEM((tokens, feats), f32),
            pltpu.VMEM((tokens + halo, feats), bf16),
            sems((6,)),
            sems((HEADS,)),
            sems((slots, peers)),
            sems((slots, peers)),
            sems((slots, peers)),
            sems((slots, peers)),
            sems((slots, max(planes // 2, 1))),
            sems((slots, rounds)),
            sems((slots, peers)),
            sems((slots, peers)),
            sems((2,)),
        ],
        compiler_params=pltpu.CompilerParams(
            collective_id=0, has_side_effects=True, vmem_limit_bytes=63 * 1024 * 1024
        ),
        cost_estimate=pl.CostEstimate(
            flops=2 * tokens * feats * feats, bytes_accessed=2 * feats * feats, transcendentals=0
        ),
        name="block_forward",
    )(query_in, key_in, value_in, hidden_in, out_weight, norm_gain, temporal_taps, block_valid)


def solution(mesh):
    split = P("frame", "row", None, None)
    placed = (split, split, split, split, P(), P(), P(), P("frame"))
    n_frame, n_row = mesh.shape["frame"], mesh.shape["row"]
    return jax.shard_map(
        functools.partial(body, n_frame, n_row),
        mesh=mesh,
        in_specs=placed,
        out_specs=split,
        check_vma=False,
    )
```

```python
import functools

import jax
import jax.numpy as jnp
from jax import lax
from jax.experimental import pallas as pl
from jax.experimental.pallas import tpu as pltpu
from jax.sharding import PartitionSpec as P

HEADS = 20
EPS_DEN = 1e-06
EPS_NORM = 1e-06
LANES = 128


def kernel(
    n_frame, n_row, group, slots,
    q_hbm, k_hbm, v_hbm, h_hbm, w_hbm, gain_hbm, taps_hbm, valid_ref,
    out_ref,
    q_in, k_in, v_in, h_in, gain_in, taps_in, w_in, kv_out, kv_all, q_out, q_all,
    state, total, state_in, state_out, att_out, att_all, res, ext,
    in_sem, w_sem, kv_send, kv_recv, q_send, q_recv, s_send, s_recv, a_send, a_recv, halo_sem,
):
    frames, rows_dev, cols, feats = q_in.shape
    tokens = frames * rows_dev * cols
    per_frame = rows_dev * cols
    dh = feats // HEADS
    peers = group * n_row
    planes = n_frame // group
    taps_n = taps_in.shape[0]
    halo = (taps_n - 1) * per_frame
    bf16, f32 = jnp.bfloat16, jnp.float32

    f, r = lax.axis_index("frame"), lax.axis_index("row")
    plane, inner = f // group, f % group
    me = inner * n_row + r

    def place(rank):
        return {"frame": plane * group + rank // n_row, "row": rank % n_row}

    def at_frame(index):
        return {"frame": index, "row": r}

    def others(step):
        return (me + step) % peers

    def first(rank):
        return (rank * HEADS + peers - 1) // peers

    def owned(rank):
        return first(rank + 1) - first(rank)

    def where_owned(rank, s, act):
        if s < HEADS // peers:
            act()
        else:
            pl.when(owned(rank) > s)(act)

    def owners(s):
        return [p for p in range(peers) if owned(p) > s]

    loads = [
        pltpu.make_async_copy(src, dst, in_sem.at[i])
        for i, (src, dst) in enumerate(
            (
                (k_hbm, k_in), (v_hbm, v_in), (q_hbm, q_in), (h_hbm, h_in),
                (gain_hbm, gain_in), (taps_hbm, taps_in),
            )
        )
    ]
    for load in loads[:3]:
        load.start()
    barrier = pltpu.get_barrier_semaphore()

    def greet(device):
        pl.semaphore_signal(barrier, inc=1, device_id=device, device_id_type=pl.DeviceIdType.MESH)

    for step in range(1, peers):
        greet(place(others(step)))
    rounds = range((planes - 1).bit_length())

    def sender(l):
        return (plane + 1) % 2 ** (l + 1) == 2**l

    def receiver(l):
        return (plane // 2**l) % 2 == 1

    partners = ()
    for l in rounds:
        partners += tuple((sender(l) & (plane + 1 + k < planes), f + (1 + k) * group) for k in range(2**l))
        partners += ((receiver(l), (plane // 2**l * 2**l - 1) * group + inner),)
    if group > 1:
        partners += (((inner == 0) & (f > 0), f - 1), ((inner == group - 1) & (f < n_frame - 1), f + 1))
    for there, index in partners:
        pl.when(there)(functools.partial(greet, at_frame(index)))

    w_loads = []
    w_first = [0]
    for s in range(slots):
        for p in owners(s):
            i = len(w_loads)
            w_loads.append(
                pltpu.make_async_copy(
                    w_hbm.at[pl.ds((first(p) + s) * dh, dh), :], w_in.at[i, pl.ds(0, dh), :], w_sem.at[i]
                )
            )
        w_first.append(len(w_loads))

    token_frame = lax.broadcasted_iota(jnp.int32, (tokens, 1), 0) // per_frame
    mask = token_frame < valid_ref[0]
    zeros = jnp.zeros((tokens, LANES - dh), bf16)
    ones = (lax.broadcasted_iota(jnp.int32, (tokens, LANES - dh), 1) == 0).astype(f32).astype(bf16)

    def put(dst, s, low, value, tail):
        for p in owners(s):
            h = first(p) + s
            dst[s, p, low : low + tokens] = jnp.concatenate([value[:, h * dh : (h + 1) * dh], tail], axis=1)

    def feature(ref):
        return jnp.where(mask, jnp.maximum(ref[...].astype(f32).reshape(tokens, feats), 0.0), 0.0).astype(bf16)

    class Exchange:
        def __init__(self, out, all_, send, recv):
            self.refs = out, all_, send, recv

        def copy(self, s, step):
            out, all_, send, recv = self.refs
            return pltpu.make_async_remote_copy(
                src_ref=out.at[s, others(step)],
                dst_ref=all_.at[s, me],
                send_sem=send.at[s, step],
                recv_sem=recv.at[s, step],
                device_id=place(others(step)),
                device_id_type=pl.DeviceIdType.MESH,
            )

        def start(self, s):
            out, all_, _, _ = self.refs
            for step in range(1, peers):
                where_owned(others(step), s, lambda step=step: self.copy(s, step).start())

            def keep():
                all_[s, pl.ds(me, 1)] = out[s, pl.ds(me, 1)]

            where_owned(me, s, keep)

        def arrived(self, s):
            for step in range(1, peers):
                self.copy(s, step).wait_recv()

        def sent(self, s):
            for step in range(1, peers):
                where_owned(others(step), s, lambda step=step: self.copy(s, step).wait_send())

    kv = Exchange(kv_out, kv_all, kv_send, kv_recv)
    query = Exchange(q_out, q_all, q_send, q_recv)

    loads[0].wait()
    key_feat = feature(k_in)
    loads[1].wait()
    value_feat = v_in[...].astype(f32).reshape(tokens, feats).astype(bf16)
    for s in range(slots):
        put(kv_out, s, 0, key_feat, zeros)
        put(kv_out, s, tokens, value_feat, ones)
        if s == 0:
            near = sum(there.astype(jnp.int32) for there, _ in partners)
            pl.semaphore_wait(barrier, peers - 1 + near)
        kv.start(s)
    loads[2].wait()
    query_feat = feature(q_in)
    for s in range(slots):
        put(q_out, s, 0, query_feat, zeros)
    def pass_on(s, l, k):
        return pltpu.make_async_remote_copy(
            src_ref=state_out.at[s],
            dst_ref=state_in.at[s, l],
            send_sem=s_send.at[s, k],
            recv_sem=s_recv.at[s, l],
            device_id=at_frame(f + (1 + k) * group),
            device_id_type=pl.DeviceIdType.MESH,
        )

    def each_target(s, l, act):
        for k in reversed(range(2**l)):
            pl.when(sender(l) & (plane + 1 + k < planes))(lambda k=k: act(pass_on(s, l, k)))

    def send_state(s, l, value):
        @pl.when(sender(l))
        def _():
            state_out[s] = value.astype(bf16)

        each_target(s, l, lambda copy: copy.start())

    def ranks(g):
        return slice(g * n_row, (g + 1) * n_row)

    def plane_state(s):
        kv.arrived(s)
        mine = []
        for g in range(group):
            keys = kv_all[s, ranks(g), 0:tokens].reshape(n_row * tokens, LANES)
            values = kv_all[s, ranks(g), tokens : 2 * tokens].reshape(n_row * tokens, LANES)
            mine.append(
                lax.dot_general(
                    keys, values, (((0,), (0,)), ((), ())), preferred_element_type=f32
                )[:dh]
            )
            state[s, g] = mine[-1]

        send_state(s, 0, sum(mine[1:], mine[0]))

    def chain(s):
        running = jnp.zeros((dh, LANES), f32)
        here = [state[s, g] for g in range(group)]
        for l in rounds:
            if l > 0:
                send_state(s, l, sum(here, running))

            @pl.when(receiver(l))
            def _():
                pass_on(s, l, 0).wait_recv()

            @pl.when(jnp.logical_not(receiver(l)))
            def _():
                state_in[s, l] = jnp.zeros((dh, LANES), bf16)

            running = running + state_in[s, l].astype(f32)
        for g in range(group):
            running = running + here[g]
            total[s, g] = running.astype(bf16)

    back = Exchange(att_out, att_all, a_send, a_recv)

    def attend(s):
        query.arrived(s)
        for g in range(group):
            queries = q_all[s, ranks(g)].reshape(n_row * tokens, LANES)[:, :dh]
            both = jnp.dot(queries, total[s, g], preferred_element_type=f32)
            value = both / (both[:, dh : dh + 1] + EPS_DEN)
            att_out[s, ranks(g)] = value.astype(bf16).reshape(n_row, tokens, LANES)

    def give_back(s):
        def mine():
            attend(s)
            for step in range(1, peers):
                back_copy(s, step).start()
            att_all[s, pl.ds(me, 1)] = att_out[s, pl.ds(me, 1)]

        where_owned(me, s, mine)

    def back_copy(s, step):
        return back.copy(s, step)

    relays = functools.reduce(jnp.logical_or, [sender(l) for l in rounds[1:]], plane < 0)

    def forward(s, when):
        pl.when(when)(lambda: where_owned(me, s, lambda: chain(s)))

    for s in range(slots):
        where_owned(me, s, lambda s=s: plane_state(s))
        if s == 0:
            for later in range(slots):
                query.start(later)
            for load in w_loads + loads[3:]:
                load.start()
            w_in[:, dh:, :] = jnp.zeros((HEADS, LANES - dh, feats), bf16)
        else:
            forward(s - 1, relays)
    forward(slots - 1, relays)
    for s in range(slots):
        forward(s, jnp.logical_not(relays))
        give_back(s)

    loads[3].wait()
    half = -(-feats // (2 * LANES)) * LANES
    square = jnp.zeros((tokens, 1), f32)
    for s in range(slots):
        here = owners(s)
        for load in w_loads[w_first[s] : w_first[s + 1]]:
            load.wait()
        for step in range(1, peers):
            where_owned((me + peers - step) % peers, s, lambda step=step: back_copy(s, step).wait_recv())
        att = jnp.concatenate([att_all[s, p] for p in here], axis=1)
        depth = len(here) * LANES
        for low, high in ((0, half), (half, feats)):
            weights = w_in[w_first[s] : w_first[s + 1], :, low:high].reshape(depth, high - low)
            summed = jnp.dot(att, weights, preferred_element_type=f32)
            if s > 0:
                summed = res[:, low:high] + summed
            if s == slots - 1:
                hidden = h_in[:, :, :, low:high].astype(f32).reshape(tokens, high - low)
                summed = (hidden + summed).astype(bf16).astype(f32)
                square = square + jnp.sum(summed * summed, axis=1, keepdims=True)
            res[:, low:high] = summed
    inverse = lax.rsqrt(square / feats + EPS_NORM)
    loads[4].wait()
    gain = gain_in[...].reshape(1, feats)
    ext[halo:, :] = (res[...] * inverse * gain).astype(bf16)

    to_next = pltpu.make_async_remote_copy(
        src_ref=ext.at[pl.ds(tokens, halo), :],
        dst_ref=ext.at[pl.ds(0, halo), :],
        send_sem=halo_sem.at[0],
        recv_sem=halo_sem.at[1],
        device_id=at_frame(f + 1),
        device_id_type=pl.DeviceIdType.MESH,
    )
    pl.when(f < n_frame - 1)(lambda: to_next.start())

    @pl.when(f == 0)
    def _():
        ext[0:halo, :] = jnp.zeros((halo, feats), bf16)

    for s in range(slots):
        kv.sent(s)
        query.sent(s)

        def gone(s=s):
            for step in range(1, peers):
                back_copy(s, step).wait_send()
            for l in rounds:
                each_target(s, l, lambda copy: copy.wait_send())

        where_owned(me, s, gone)
    loads[5].wait()
    pl.when(f > 0)(lambda: to_next.wait_recv())
    normed = ext[...].astype(f32)
    taps = taps_in[...]
    temporal = jnp.zeros((tokens, feats), f32)
    for j in range(taps_n):
        low = (taps_n - 1 - j) * per_frame
        temporal = temporal + taps[j : j + 1] * normed[low : low + tokens]
    mixed = res[...] + temporal.astype(bf16).astype(f32)
    out_ref[...] = mixed.reshape(out_ref.shape).astype(bf16)
    pl.when(f < n_frame - 1)(lambda: to_next.wait_send())


def body(n_frame, n_row, query_in, key_in, value_in, hidden_in, out_weight, norm_gain, temporal_taps, block_valid):
    frames, rows_dev, cols, feats = query_in.shape
    tokens = frames * rows_dev * cols
    group = 2 if n_frame % 2 == 0 else 1
    peers = group * n_row
    slots = -(-HEADS // peers)
    planes = n_frame // group
    rounds = max((planes - 1).bit_length(), 1)
    dh = feats // HEADS
    halo = (temporal_taps.shape[0] - 1) * rows_dev * cols
    bf16, f32 = jnp.bfloat16, jnp.float32
    hbm = pl.BlockSpec(memory_space=pltpu.HBM)
    vmem = pl.BlockSpec(memory_space=pltpu.VMEM)
    smem = pl.BlockSpec(memory_space=pltpu.SMEM)
    sems = pltpu.SemaphoreType.DMA
    return pl.pallas_call(
        functools.partial(kernel, n_frame, n_row, group, slots),
        out_shape=jax.ShapeDtypeStruct(query_in.shape, bf16),
        in_specs=[hbm] * 7 + [smem],
        out_specs=vmem,
        scratch_shapes=[
            pltpu.VMEM(query_in.shape, bf16),
            pltpu.VMEM(query_in.shape, bf16),
            pltpu.VMEM(query_in.shape, bf16),
            pltpu.VMEM(query_in.shape, bf16),
            pltpu.VMEM(norm_gain.shape, f32),
            pltpu.VMEM(temporal_taps.shape, f32),
            pltpu.VMEM((HEADS, LANES, feats), bf16),
            pltpu.VMEM((slots, peers, 2 * tokens, LANES), bf16),
            pltpu.VMEM((slots, peers, 2 * tokens, LANES), bf16),
            pltpu.VMEM((slots, peers, tokens, LANES), bf16),
            pltpu.VMEM((slots, peers, tokens, LANES), bf16),
            pltpu.VMEM((slots, group, dh, LANES), f32),
            pltpu.VMEM((slots, group, dh, LANES), bf16),
            pltpu.VMEM((slots, rounds, dh, LANES), bf16),
            pltpu.VMEM((slots, dh, LANES), bf16),
            pltpu.VMEM((slots, peers, tokens, LANES), bf16),
            pltpu.VMEM((slots, peers, tokens, LANES), bf16),
            pltpu.VMEM((tokens, feats), f32),
            pltpu.VMEM((tokens + halo, feats), bf16),
            sems((6,)),
            sems((HEADS,)),
            sems((slots, peers)),
            sems((slots, peers)),
            sems((slots, peers)),
            sems((slots, peers)),
            sems((slots, max(planes // 2, 1))),
            sems((slots, rounds)),
            sems((slots, peers)),
            sems((slots, peers)),
            sems((2,)),
        ],
        compiler_params=pltpu.CompilerParams(
            collective_id=0, has_side_effects=True, vmem_limit_bytes=63 * 1024 * 1024
        ),
        cost_estimate=pl.CostEstimate(
            flops=2 * tokens * feats * feats, bytes_accessed=2 * feats * feats, transcendentals=0
        ),
        name="block_forward",
    )(query_in, key_in, value_in, hidden_in, out_weight, norm_gain, temporal_taps, block_valid)


def solution(mesh):
    split = P("frame", "row", None, None)
    placed = (split, split, split, split, P(), P(), P(), P("frame"))
    n_frame, n_row = mesh.shape["frame"], mesh.shape["row"]
    return jax.shard_map(
        functools.partial(body, n_frame, n_row),
        mesh=mesh,
        in_specs=placed,
        out_specs=split,
        check_vma=False,
    )
```

```python
import functools

import jax
import jax.numpy as jnp
from jax import lax
from jax.experimental import pallas as pl
from jax.experimental.pallas import tpu as pltpu
from jax.sharding import PartitionSpec as P

HEADS = 20
EPS_DEN = 1e-06
EPS_NORM = 1e-06
LANES = 128


def kernel(
    n_frame, n_row, group, slots,
    q_hbm, k_hbm, v_hbm, h_hbm, w_hbm, gain_hbm, taps_hbm, valid_ref,
    out_ref,
    q_in, k_in, v_in, h_in, gain_in, taps_in, w_in, kv_out, kv_all, q_out, q_all,
    state, total, state_in, state_out, att_out, att_all, res, ext,
    in_sem, w_sem, kv_send, kv_recv, q_send, q_recv, s_send, s_recv, a_send, a_recv, halo_sem,
):
    frames, rows_dev, cols, feats = q_in.shape
    tokens = frames * rows_dev * cols
    per_frame = rows_dev * cols
    dh = feats // HEADS
    peers = group * n_row
    planes = n_frame // group
    taps_n = taps_in.shape[0]
    halo = (taps_n - 1) * per_frame
    bf16, f32 = jnp.bfloat16, jnp.float32

    f, r = lax.axis_index("frame"), lax.axis_index("row")
    plane, inner = f // group, f % group
    me = inner * n_row + r

    def place(rank):
        return {"frame": plane * group + rank // n_row, "row": rank % n_row}

    def at_frame(index):
        return {"frame": index, "row": r}

    def others(step):
        return (me + step) % peers

    def first(rank):
        return (rank * HEADS + peers - 1) // peers

    def owned(rank):
        return first(rank + 1) - first(rank)

    def where_owned(rank, s, act):
        if s < HEADS // peers:
            act()
        else:
            pl.when(owned(rank) > s)(act)

    def owners(s):
        return [p for p in range(peers) if owned(p) > s]

    loads = [
        pltpu.make_async_copy(src, dst, in_sem.at[i])
        for i, (src, dst) in enumerate(
            (
                (k_hbm, k_in), (v_hbm, v_in), (q_hbm, q_in), (h_hbm, h_in),
                (gain_hbm, gain_in), (taps_hbm, taps_in),
            )
        )
    ]
    for load in loads[:3]:
        load.start()
    barrier = pltpu.get_barrier_semaphore()

    def greet(device):
        pl.semaphore_signal(barrier, inc=1, device_id=device, device_id_type=pl.DeviceIdType.MESH)

    for step in range(1, peers):
        greet(place(others(step)))
    rounds = range((planes - 1).bit_length())

    def sender(l):
        return (plane + 1) % 2 ** (l + 1) == 2**l

    def receiver(l):
        return (plane // 2**l) % 2 == 1

    partners = ()
    for l in rounds:
        partners += tuple((sender(l) & (plane + 1 + k < planes), f + (1 + k) * group) for k in range(2**l))
        partners += ((receiver(l), (plane // 2**l * 2**l - 1) * group + inner),)
    if group > 1:
        partners += (((inner == 0) & (f > 0), f - 1), ((inner == group - 1) & (f < n_frame - 1), f + 1))
    for there, index in partners:
        pl.when(there)(functools.partial(greet, at_frame(index)))

    w_loads = []
    w_first = [0]
    for s in range(slots):
        for p in owners(s):
            i = len(w_loads)
            w_loads.append(
                pltpu.make_async_copy(
                    w_hbm.at[pl.ds((first(p) + s) * dh, dh), :], w_in.at[i, pl.ds(0, dh), :], w_sem.at[i]
                )
            )
        w_first.append(len(w_loads))

    token_frame = lax.broadcasted_iota(jnp.int32, (tokens, 1), 0) // per_frame
    mask = token_frame < valid_ref[0]
    zeros = jnp.zeros((tokens, LANES - dh), bf16)
    ones = (lax.broadcasted_iota(jnp.int32, (tokens, LANES - dh), 1) == 0).astype(f32).astype(bf16)

    def put(dst, s, low, value, tail):
        for p in owners(s):
            h = first(p) + s
            dst[s, p, low : low + tokens] = jnp.concatenate([value[:, h * dh : (h + 1) * dh], tail], axis=1)

    def feature(ref):
        return jnp.where(mask, jnp.maximum(ref[...].astype(f32).reshape(tokens, feats), 0.0), 0.0).astype(bf16)

    class Exchange:
        def __init__(self, out, all_, send, recv):
            self.refs = out, all_, send, recv

        def copy(self, s, step):
            out, all_, send, recv = self.refs
            return pltpu.make_async_remote_copy(
                src_ref=out.at[s, others(step)],
                dst_ref=all_.at[s, me],
                send_sem=send.at[s, step],
                recv_sem=recv.at[s, step],
                device_id=place(others(step)),
                device_id_type=pl.DeviceIdType.MESH,
            )

        def start(self, s):
            out, all_, _, _ = self.refs
            for step in range(1, peers):
                where_owned(others(step), s, lambda step=step: self.copy(s, step).start())

            def keep():
                all_[s, pl.ds(me, 1)] = out[s, pl.ds(me, 1)]

            where_owned(me, s, keep)

        def arrived(self, s):
            for step in range(1, peers):
                self.copy(s, step).wait_recv()

        def sent(self, s):
            for step in range(1, peers):
                where_owned(others(step), s, lambda step=step: self.copy(s, step).wait_send())

    kv = Exchange(kv_out, kv_all, kv_send, kv_recv)
    query = Exchange(q_out, q_all, q_send, q_recv)

    loads[0].wait()
    key_feat = feature(k_in)
    loads[1].wait()
    value_feat = v_in[...].astype(f32).reshape(tokens, feats).astype(bf16)
    for s in range(slots):
        put(kv_out, s, 0, key_feat, zeros)
        put(kv_out, s, tokens, value_feat, ones)
        if s == 0:
            near = sum(there.astype(jnp.int32) for there, _ in partners)
            pl.semaphore_wait(barrier, peers - 1 + near)
        kv.start(s)
    loads[2].wait()
    query_feat = feature(q_in)
    for s in range(slots):
        put(q_out, s, 0, query_feat, zeros)
    def pass_on(s, l, k):
        return pltpu.make_async_remote_copy(
            src_ref=state_out.at[s],
            dst_ref=state_in.at[s, l],
            send_sem=s_send.at[s, k],
            recv_sem=s_recv.at[s, l],
            device_id=at_frame(f + (1 + k) * group),
            device_id_type=pl.DeviceIdType.MESH,
        )

    def each_target(s, l, act):
        for k in reversed(range(2**l)):
            pl.when(sender(l) & (plane + 1 + k < planes))(lambda k=k: act(pass_on(s, l, k)))

    def send_state(s, l, value):
        @pl.when(sender(l))
        def _():
            state_out[s] = value.astype(bf16)

        each_target(s, l, lambda copy: copy.start())

    def ranks(g):
        return slice(g * n_row, (g + 1) * n_row)

    def plane_state(s):
        kv.arrived(s)
        mine = []
        for g in range(group):
            keys = kv_all[s, ranks(g), 0:tokens].reshape(n_row * tokens, LANES)
            values = kv_all[s, ranks(g), tokens : 2 * tokens].reshape(n_row * tokens, LANES)
            mine.append(
                lax.dot_general(
                    keys, values, (((0,), (0,)), ((), ())), preferred_element_type=f32
                )[:dh]
            )
            state[s, g] = mine[-1]

        send_state(s, 0, sum(mine[1:], mine[0]))

    def chain(s):
        running = jnp.zeros((dh, LANES), f32)
        here = [state[s, g] for g in range(group)]
        for l in rounds:
            if l > 0:
                send_state(s, l, sum(here, running))

            @pl.when(receiver(l))
            def _():
                pass_on(s, l, 0).wait_recv()

            @pl.when(jnp.logical_not(receiver(l)))
            def _():
                state_in[s, l] = jnp.zeros((dh, LANES), bf16)

            running = running + state_in[s, l].astype(f32)
        for g in range(group):
            running = running + here[g]
            total[s, g] = running.astype(bf16)

    back = Exchange(att_out, att_all, a_send, a_recv)

    def attend(s):
        query.arrived(s)
        for g in range(group):
            queries = q_all[s, ranks(g)].reshape(n_row * tokens, LANES)[:, :dh]
            both = jnp.dot(queries, total[s, g], preferred_element_type=f32)
            value = both / (both[:, dh : dh + 1] + EPS_DEN)
            att_out[s, ranks(g)] = value.astype(bf16).reshape(n_row, tokens, LANES)

    def give_back(s):
        def mine():
            attend(s)
            for step in range(1, peers):
                back_copy(s, step).start()
            att_all[s, pl.ds(me, 1)] = att_out[s, pl.ds(me, 1)]

        where_owned(me, s, mine)

    def back_copy(s, step):
        return back.copy(s, step)

    relays = functools.reduce(jnp.logical_or, [sender(l) for l in rounds[1:]], plane < 0)

    def forward(s, when):
        pl.when(when)(lambda: where_owned(me, s, lambda: chain(s)))

    for s in range(slots):
        where_owned(me, s, lambda s=s: plane_state(s))
        if s == 0:
            for later in range(slots):
                query.start(later)
            for load in w_loads + loads[3:]:
                load.start()
            w_in[:, dh:, :] = jnp.zeros((HEADS, LANES - dh, feats), bf16)
        else:
            forward(s - 1, relays)
    forward(slots - 1, relays)
    for s in range(slots):
        forward(s, jnp.logical_not(relays))
        give_back(s)

    loads[3].wait()
    half = -(-feats // (2 * LANES)) * LANES
    square = jnp.zeros((tokens, 1), f32)
    for s in range(slots):
        here = owners(s)
        for load in w_loads[w_first[s] : w_first[s + 1]]:
            load.wait()
        for step in range(1, peers):
            where_owned((me + peers - step) % peers, s, lambda step=step: back_copy(s, step).wait_recv())
        att = jnp.concatenate([att_all[s, p] for p in here], axis=1)
        depth = len(here) * LANES
        for low, high in ((0, half), (half, feats)):
            weights = w_in[w_first[s] : w_first[s + 1], :, low:high].reshape(depth, high - low)
            summed = jnp.dot(att, weights, preferred_element_type=f32)
            if s > 0:
                summed = res[:, low:high] + summed
            if s == slots - 1:
                hidden = h_in[:, :, :, low:high].astype(f32).reshape(tokens, high - low)
                summed = (hidden + summed).astype(bf16).astype(f32)
                square = square + jnp.sum(summed * summed, axis=1, keepdims=True)
            res[:, low:high] = summed
    inverse = lax.rsqrt(square / feats + EPS_NORM)
    loads[4].wait()
    gain = gain_in[...].reshape(1, feats)
    ext[halo:, :] = (res[...] * inverse * gain).astype(bf16)

    to_next = pltpu.make_async_remote_copy(
        src_ref=ext.at[pl.ds(tokens, halo), :],
        dst_ref=ext.at[pl.ds(0, halo), :],
        send_sem=halo_sem.at[0],
        recv_sem=halo_sem.at[1],
        device_id=at_frame(f + 1),
        device_id_type=pl.DeviceIdType.MESH,
    )
    pl.when(f < n_frame - 1)(lambda: to_next.start())

    @pl.when(f == 0)
    def _():
        ext[0:halo, :] = jnp.zeros((halo, feats), bf16)

    loads[5].wait()
    taps = taps_in[...]

    def mix(low, high):
        normed = ext[low : high + halo, :].astype(f32)
        temporal = jnp.zeros((high - low, feats), f32)
        for j in range(taps_n):
            start = (taps_n - 1 - j) * per_frame
            temporal = temporal + taps[j : j + 1] * normed[start : start + high - low]
        mixed = res[low:high, :] + temporal.astype(bf16).astype(f32)
        count = (high - low) // per_frame
        out_ref[low // per_frame : high // per_frame] = mixed.reshape(count, rows_dev, cols, feats)

    if tokens > halo:
        mix(halo, tokens)
    for s in range(slots):
        kv.sent(s)
        query.sent(s)

        def gone(s=s):
            for step in range(1, peers):
                back_copy(s, step).wait_send()
            for l in rounds:
                each_target(s, l, lambda copy: copy.wait_send())

        where_owned(me, s, gone)
    pl.when(f > 0)(lambda: to_next.wait_recv())
    mix(0, min(halo, tokens))
    pl.when(f < n_frame - 1)(lambda: to_next.wait_send())


def body(n_frame, n_row, query_in, key_in, value_in, hidden_in, out_weight, norm_gain, temporal_taps, block_valid):
    frames, rows_dev, cols, feats = query_in.shape
    tokens = frames * rows_dev * cols
    group = 2 if n_frame % 2 == 0 else 1
    peers = group * n_row
    slots = -(-HEADS // peers)
    planes = n_frame // group
    rounds = max((planes - 1).bit_length(), 1)
    dh = feats // HEADS
    halo = (temporal_taps.shape[0] - 1) * rows_dev * cols
    bf16, f32 = jnp.bfloat16, jnp.float32
    hbm = pl.BlockSpec(memory_space=pltpu.HBM)
    vmem = pl.BlockSpec(memory_space=pltpu.VMEM)
    smem = pl.BlockSpec(memory_space=pltpu.SMEM)
    sems = pltpu.SemaphoreType.DMA
    mixed = pl.pallas_call(
        functools.partial(kernel, n_frame, n_row, group, slots),
        out_shape=jax.ShapeDtypeStruct(query_in.shape, f32),
        in_specs=[hbm] * 7 + [smem],
        out_specs=vmem,
        scratch_shapes=[
            pltpu.VMEM(query_in.shape, bf16),
            pltpu.VMEM(query_in.shape, bf16),
            pltpu.VMEM(query_in.shape, bf16),
            pltpu.VMEM(query_in.shape, bf16),
            pltpu.VMEM(norm_gain.shape, f32),
            pltpu.VMEM(temporal_taps.shape, f32),
            pltpu.VMEM((HEADS, LANES, feats), bf16),
            pltpu.VMEM((slots, peers, 2 * tokens, LANES), bf16),
            pltpu.VMEM((slots, peers, 2 * tokens, LANES), bf16),
            pltpu.VMEM((slots, peers, tokens, LANES), bf16),
            pltpu.VMEM((slots, peers, tokens, LANES), bf16),
            pltpu.VMEM((slots, group, dh, LANES), f32),
            pltpu.VMEM((slots, group, dh, LANES), bf16),
            pltpu.VMEM((slots, rounds, dh, LANES), bf16),
            pltpu.VMEM((slots, dh, LANES), bf16),
            pltpu.VMEM((slots, peers, tokens, LANES), bf16),
            pltpu.VMEM((slots, peers, tokens, LANES), bf16),
            pltpu.VMEM((tokens, feats), f32),
            pltpu.VMEM((tokens + halo, feats), bf16),
            sems((6,)),
            sems((HEADS,)),
            sems((slots, peers)),
            sems((slots, peers)),
            sems((slots, peers)),
            sems((slots, peers)),
            sems((slots, max(planes // 2, 1))),
            sems((slots, rounds)),
            sems((slots, peers)),
            sems((slots, peers)),
            sems((2,)),
        ],
        compiler_params=pltpu.CompilerParams(
            collective_id=0, has_side_effects=True, vmem_limit_bytes=63 * 1024 * 1024
        ),
        cost_estimate=pl.CostEstimate(
            flops=2 * tokens * feats * feats, bytes_accessed=2 * feats * feats, transcendentals=0
        ),
        name="block_forward",
    )(query_in, key_in, value_in, hidden_in, out_weight, norm_gain, temporal_taps, block_valid)
    return mixed.astype(bf16)


def solution(mesh):
    split = P("frame", "row", None, None)
    placed = (split, split, split, split, P(), P(), P(), P("frame"))
    n_frame, n_row = mesh.shape["frame"], mesh.shape["row"]
    return jax.shard_map(
        functools.partial(body, n_frame, n_row),
        mesh=mesh,
        in_specs=placed,
        out_specs=split,
        check_vma=False,
    )
```

```python
import functools

import jax
import jax.numpy as jnp
from jax import lax
from jax.experimental import pallas as pl
from jax.experimental.pallas import tpu as pltpu
from jax.sharding import PartitionSpec as P

HEADS = 20
EPS_DEN = 1e-06
EPS_NORM = 1e-06
LANES = 128


def kernel(
    n_frame, n_row, group, slots,
    q_hbm, k_hbm, v_hbm, h_hbm, w_hbm, gain_hbm, taps_hbm, valid_ref,
    out_ref,
    q_in, k_in, v_in, h_in, gain_in, taps_in, w_in, kv_out, kv_all, q_out, q_all,
    state, total, state_in, state_out, att_out, att_all, res, ext,
    in_sem, w_sem, kv_send, kv_recv, q_send, q_recv, s_send, s_recv, a_send, a_recv, halo_sem,
):
    frames, rows_dev, cols, feats = q_in.shape
    tokens = frames * rows_dev * cols
    per_frame = rows_dev * cols
    dh = feats // HEADS
    peers = group * n_row
    planes = n_frame // group
    taps_n = taps_in.shape[0]
    halo = (taps_n - 1) * per_frame
    bf16, f32 = jnp.bfloat16, jnp.float32

    f, r = lax.axis_index("frame"), lax.axis_index("row")
    plane, inner = f // group, f % group
    me = inner * n_row + r

    def place(rank):
        return {"frame": plane * group + rank // n_row, "row": rank % n_row}

    def at_frame(index):
        return {"frame": index, "row": r}

    def others(step):
        return (me + step) % peers

    def first(rank):
        return (rank * HEADS + peers - 1) // peers

    def owned(rank):
        return first(rank + 1) - first(rank)

    def where_owned(rank, s, act):
        if s < HEADS // peers:
            act()
        else:
            pl.when(owned(rank) > s)(act)

    def owners(s):
        return [p for p in range(peers) if owned(p) > s]

    loads = [
        pltpu.make_async_copy(src, dst, in_sem.at[i])
        for i, (src, dst) in enumerate(
            (
                (k_hbm, k_in), (v_hbm, v_in), (q_hbm, q_in), (h_hbm, h_in),
                (gain_hbm, gain_in), (taps_hbm, taps_in),
            )
        )
    ]
    for load in loads[:2]:
        load.start()
    barrier = pltpu.get_barrier_semaphore()

    def greet(device):
        pl.semaphore_signal(barrier, inc=1, device_id=device, device_id_type=pl.DeviceIdType.MESH)

    for step in range(1, peers):
        greet(place(others(step)))
    rounds = range((planes - 1).bit_length())

    def sender(l):
        return (plane + 1) % 2 ** (l + 1) == 2**l

    def receiver(l):
        return (plane // 2**l) % 2 == 1

    partners = ()
    for l in rounds:
        partners += tuple((sender(l) & (plane + 1 + k < planes), f + (1 + k) * group) for k in range(2**l))
        partners += ((receiver(l), (plane // 2**l * 2**l - 1) * group + inner),)
    if group > 1:
        partners += (((inner == 0) & (f > 0), f - 1), ((inner == group - 1) & (f < n_frame - 1), f + 1))
    for there, index in partners:
        pl.when(there)(functools.partial(greet, at_frame(index)))

    loads[2].start()
    w_loads = []
    w_first = [0]
    for s in range(slots):
        for p in owners(s):
            i = len(w_loads)
            w_loads.append(
                pltpu.make_async_copy(
                    w_hbm.at[pl.ds((first(p) + s) * dh, dh), :], w_in.at[i, pl.ds(0, dh), :], w_sem.at[i]
                )
            )
        w_first.append(len(w_loads))

    token_frame = lax.broadcasted_iota(jnp.int32, (tokens, 1), 0) // per_frame
    mask = token_frame < valid_ref[0]
    zeros = jnp.zeros((tokens, LANES - dh), bf16)
    ones = (lax.broadcasted_iota(jnp.int32, (tokens, LANES - dh), 1) == 0).astype(f32).astype(bf16)

    def put(dst, s, low, value, tail):
        for p in owners(s):
            h = first(p) + s
            dst[s, p, low : low + tokens] = jnp.concatenate([value[:, h * dh : (h + 1) * dh], tail], axis=1)

    def feature(ref):
        return jnp.where(mask, jnp.maximum(ref[...].astype(f32).reshape(tokens, feats), 0.0), 0.0).astype(bf16)

    class Exchange:
        def __init__(self, out, all_, send, recv):
            self.refs = out, all_, send, recv

        def copy(self, s, step):
            out, all_, send, recv = self.refs
            return pltpu.make_async_remote_copy(
                src_ref=out.at[s, others(step)],
                dst_ref=all_.at[s, me],
                send_sem=send.at[s, step],
                recv_sem=recv.at[s, step],
                device_id=place(others(step)),
                device_id_type=pl.DeviceIdType.MESH,
            )

        def start(self, s):
            out, all_, _, _ = self.refs
            for step in range(1, peers):
                where_owned(others(step), s, lambda step=step: self.copy(s, step).start())

            def keep():
                all_[s, pl.ds(me, 1)] = out[s, pl.ds(me, 1)]

            where_owned(me, s, keep)

        def arrived(self, s):
            for step in range(1, peers):
                self.copy(s, step).wait_recv()

        def sent(self, s):
            for step in range(1, peers):
                where_owned(others(step), s, lambda step=step: self.copy(s, step).wait_send())

    kv = Exchange(kv_out, kv_all, kv_send, kv_recv)
    query = Exchange(q_out, q_all, q_send, q_recv)

    loads[0].wait()
    key_feat = feature(k_in)
    loads[1].wait()
    value_feat = v_in[...].astype(f32).reshape(tokens, feats).astype(bf16)
    for s in range(slots):
        put(kv_out, s, 0, key_feat, zeros)
        put(kv_out, s, tokens, value_feat, ones)
        if s == 0:
            near = sum(there.astype(jnp.int32) for there, _ in partners)
            pl.semaphore_wait(barrier, peers - 1 + near)
        kv.start(s)
    loads[2].wait()
    query_feat = feature(q_in)
    for s in range(slots):
        put(q_out, s, 0, query_feat, zeros)
    def pass_on(s, l, k):
        return pltpu.make_async_remote_copy(
            src_ref=state_out.at[s],
            dst_ref=state_in.at[s, l],
            send_sem=s_send.at[s, k],
            recv_sem=s_recv.at[s, l],
            device_id=at_frame(f + (1 + k) * group),
            device_id_type=pl.DeviceIdType.MESH,
        )

    def each_target(s, l, act):
        for k in reversed(range(2**l)):
            pl.when(sender(l) & (plane + 1 + k < planes))(lambda k=k: act(pass_on(s, l, k)))

    def send_state(s, l, value):
        @pl.when(sender(l))
        def _():
            state_out[s] = value.astype(bf16)

        each_target(s, l, lambda copy: copy.start())

    def ranks(g):
        return slice(g * n_row, (g + 1) * n_row)

    def plane_state(s):
        kv.arrived(s)
        mine = []
        for g in range(group):
            keys = kv_all[s, ranks(g), 0:tokens].reshape(n_row * tokens, LANES)
            values = kv_all[s, ranks(g), tokens : 2 * tokens].reshape(n_row * tokens, LANES)
            mine.append(
                lax.dot_general(
                    keys, values, (((0,), (0,)), ((), ())), preferred_element_type=f32
                )[:dh]
            )
            state[s, g] = mine[-1]

        send_state(s, 0, sum(mine[1:], mine[0]))

    def chain(s):
        running = jnp.zeros((dh, LANES), f32)
        here = [state[s, g] for g in range(group)]
        for l in rounds:
            if l > 0:
                send_state(s, l, sum(here, running))

            @pl.when(receiver(l))
            def _():
                pass_on(s, l, 0).wait_recv()

            @pl.when(jnp.logical_not(receiver(l)))
            def _():
                state_in[s, l] = jnp.zeros((dh, LANES), bf16)

            running = running + state_in[s, l].astype(f32)
        for g in range(group):
            running = running + here[g]
            total[s, g] = running.astype(bf16)

    back = Exchange(att_out, att_all, a_send, a_recv)

    def attend(s):
        query.arrived(s)
        for g in range(group):
            queries = q_all[s, ranks(g)].reshape(n_row * tokens, LANES)[:, :dh]
            both = jnp.dot(queries, total[s, g], preferred_element_type=f32)
            value = both / (both[:, dh : dh + 1] + EPS_DEN)
            att_out[s, ranks(g)] = value.astype(bf16).reshape(n_row, tokens, LANES)

    def give_back(s):
        def mine():
            attend(s)
            for step in range(1, peers):
                back_copy(s, step).start()
            att_all[s, pl.ds(me, 1)] = att_out[s, pl.ds(me, 1)]

        where_owned(me, s, mine)

    def back_copy(s, step):
        return back.copy(s, step)

    relays = functools.reduce(jnp.logical_or, [sender(l) for l in rounds[1:]], plane < 0)

    def forward(s, when):
        pl.when(when)(lambda: where_owned(me, s, lambda: chain(s)))

    for s in range(slots):
        where_owned(me, s, lambda s=s: plane_state(s))
        if s == 0:
            for later in range(slots):
                query.start(later)
            for load in w_loads + loads[3:]:
                load.start()
            w_in[:, dh:, :] = jnp.zeros((HEADS, LANES - dh, feats), bf16)
        else:
            forward(s - 1, relays)
    forward(slots - 1, relays)
    for s in range(slots):
        forward(s, jnp.logical_not(relays))
        give_back(s)

    loads[3].wait()
    half = -(-feats // (2 * LANES)) * LANES
    square = jnp.zeros((tokens, 1), f32)
    for s in range(slots):
        here = owners(s)
        for load in w_loads[w_first[s] : w_first[s + 1]]:
            load.wait()
        for step in range(1, peers):
            where_owned((me + peers - step) % peers, s, lambda step=step: back_copy(s, step).wait_recv())
        att = jnp.concatenate([att_all[s, p] for p in here], axis=1)
        depth = len(here) * LANES
        for low, high in ((0, half), (half, feats)):
            weights = w_in[w_first[s] : w_first[s + 1], :, low:high].reshape(depth, high - low)
            summed = jnp.dot(att, weights, preferred_element_type=f32)
            if s > 0:
                summed = res[:, low:high] + summed
            if s == slots - 1:
                hidden = h_in[:, :, :, low:high].astype(f32).reshape(tokens, high - low)
                summed = (hidden + summed).astype(bf16).astype(f32)
                square = square + jnp.sum(summed * summed, axis=1, keepdims=True)
            res[:, low:high] = summed
    inverse = lax.rsqrt(square / feats + EPS_NORM)
    loads[4].wait()
    gain = gain_in[...].reshape(1, feats)
    ext[tokens:, :] = (res[tokens - halo :, :] * inverse[tokens - halo :] * gain).astype(bf16)
    to_next = pltpu.make_async_remote_copy(
        src_ref=ext.at[pl.ds(tokens, halo), :],
        dst_ref=ext.at[pl.ds(0, halo), :],
        send_sem=halo_sem.at[0],
        recv_sem=halo_sem.at[1],
        device_id=at_frame(f + 1),
        device_id_type=pl.DeviceIdType.MESH,
    )
    pl.when(f < n_frame - 1)(lambda: to_next.start())
    if tokens > halo:
        ext[halo:tokens, :] = (res[: tokens - halo, :] * inverse[: tokens - halo] * gain).astype(bf16)

    @pl.when(f == 0)
    def _():
        ext[0:halo, :] = jnp.zeros((halo, feats), bf16)

    loads[5].wait()
    taps = taps_in[...]

    def mix(low, high):
        normed = ext[low : high + halo, :].astype(f32)
        temporal = jnp.zeros((high - low, feats), f32)
        for j in range(taps_n):
            start = (taps_n - 1 - j) * per_frame
            temporal = temporal + taps[j : j + 1] * normed[start : start + high - low]
        mixed = res[low:high, :] + temporal.astype(bf16).astype(f32)
        count = (high - low) // per_frame
        out_ref[low // per_frame : high // per_frame] = mixed.reshape(count, rows_dev, cols, feats).astype(bf16)

    if tokens > halo:
        mix(halo, tokens)
    for s in range(slots):
        kv.sent(s)
        query.sent(s)

        def gone(s=s):
            for step in range(1, peers):
                back_copy(s, step).wait_send()
            for l in rounds:
                each_target(s, l, lambda copy: copy.wait_send())

        where_owned(me, s, gone)
    pl.when(f > 0)(lambda: to_next.wait_recv())
    mix(0, min(halo, tokens))
    pl.when(f < n_frame - 1)(lambda: to_next.wait_send())


def body(n_frame, n_row, query_in, key_in, value_in, hidden_in, out_weight, norm_gain, temporal_taps, block_valid):
    frames, rows_dev, cols, feats = query_in.shape
    tokens = frames * rows_dev * cols
    group = 2 if n_frame % 2 == 0 else 1
    peers = group * n_row
    slots = -(-HEADS // peers)
    planes = n_frame // group
    rounds = max((planes - 1).bit_length(), 1)
    dh = feats // HEADS
    halo = (temporal_taps.shape[0] - 1) * rows_dev * cols
    bf16, f32 = jnp.bfloat16, jnp.float32
    hbm = pl.BlockSpec(memory_space=pltpu.HBM)
    vmem = pl.BlockSpec(memory_space=pltpu.VMEM)
    smem = pl.BlockSpec(memory_space=pltpu.SMEM)
    sems = pltpu.SemaphoreType.DMA
    return pl.pallas_call(
        functools.partial(kernel, n_frame, n_row, group, slots),
        out_shape=jax.ShapeDtypeStruct(query_in.shape, bf16),
        in_specs=[hbm] * 7 + [smem],
        out_specs=vmem,
        scratch_shapes=[
            pltpu.VMEM(query_in.shape, bf16),
            pltpu.VMEM(query_in.shape, bf16),
            pltpu.VMEM(query_in.shape, bf16),
            pltpu.VMEM(query_in.shape, bf16),
            pltpu.VMEM(norm_gain.shape, f32),
            pltpu.VMEM(temporal_taps.shape, f32),
            pltpu.VMEM((HEADS, LANES, feats), bf16),
            pltpu.VMEM((slots, peers, 2 * tokens, LANES), bf16),
            pltpu.VMEM((slots, peers, 2 * tokens, LANES), bf16),
            pltpu.VMEM((slots, peers, tokens, LANES), bf16),
            pltpu.VMEM((slots, peers, tokens, LANES), bf16),
            pltpu.VMEM((slots, group, dh, LANES), f32),
            pltpu.VMEM((slots, group, dh, LANES), bf16),
            pltpu.VMEM((slots, rounds, dh, LANES), bf16),
            pltpu.VMEM((slots, dh, LANES), bf16),
            pltpu.VMEM((slots, peers, tokens, LANES), bf16),
            pltpu.VMEM((slots, peers, tokens, LANES), bf16),
            pltpu.VMEM((tokens, feats), f32),
            pltpu.VMEM((tokens + halo, feats), bf16),
            sems((6,)),
            sems((HEADS,)),
            sems((slots, peers)),
            sems((slots, peers)),
            sems((slots, peers)),
            sems((slots, peers)),
            sems((slots, max(planes // 2, 1))),
            sems((slots, rounds)),
            sems((slots, peers)),
            sems((slots, peers)),
            sems((2,)),
        ],
        compiler_params=pltpu.CompilerParams(
            collective_id=0, has_side_effects=True, vmem_limit_bytes=63 * 1024 * 1024
        ),
        cost_estimate=pl.CostEstimate(
            flops=2 * tokens * feats * feats, bytes_accessed=2 * feats * feats, transcendentals=0
        ),
        name="block_forward",
    )(query_in, key_in, value_in, hidden_in, out_weight, norm_gain, temporal_taps, block_valid)


def solution(mesh):
    split = P("frame", "row", None, None)
    placed = (split, split, split, split, P(), P(), P(), P("frame"))
    n_frame, n_row = mesh.shape["frame"], mesh.shape["row"]
    return jax.shard_map(
        functools.partial(body, n_frame, n_row),
        mesh=mesh,
        in_specs=placed,
        out_specs=split,
        check_vma=False,
    )
```

```python
import functools

import jax
import jax.numpy as jnp
from jax import lax
from jax.experimental import pallas as pl
from jax.experimental.pallas import tpu as pltpu
from jax.sharding import PartitionSpec as P

HEADS = 20
EPS_DEN = 1e-06
EPS_NORM = 1e-06
LANES = 128


def kernel(
    n_frame, n_row, group, slots,
    q_hbm, k_hbm, v_hbm, h_hbm, w_hbm, gain_hbm, taps_hbm, valid_ref,
    out_ref,
    q_in, k_in, v_in, h_in, gain_in, taps_in, w_in, kv_out, kv_all, q_out, q_all,
    state, total, state_in, state_out, att_out, att_all, res, ext,
    in_sem, w_sem, kv_send, kv_recv, q_send, q_recv, s_send, s_recv, a_send, a_recv, halo_sem,
):
    frames, rows_dev, cols, feats = q_in.shape
    tokens = frames * rows_dev * cols
    per_frame = rows_dev * cols
    dh = feats // HEADS
    peers = group * n_row
    planes = n_frame // group
    taps_n = taps_in.shape[0]
    halo = (taps_n - 1) * per_frame
    bf16, f32 = jnp.bfloat16, jnp.float32

    f, r = lax.axis_index("frame"), lax.axis_index("row")
    plane, inner = f // group, f % group
    me = inner * n_row + r

    def place(rank):
        return {"frame": plane * group + rank // n_row, "row": rank % n_row}

    def at_frame(index):
        return {"frame": index, "row": r}

    def others(step):
        return (me + step) % peers

    def first(rank):
        return (rank * HEADS + peers - 1) // peers

    def owned(rank):
        return first(rank + 1) - first(rank)

    def where_owned(rank, s, act):
        if s < HEADS // peers:
            act()
        else:
            pl.when(owned(rank) > s)(act)

    def owners(s):
        return [p for p in range(peers) if owned(p) > s]

    loads = [
        pltpu.make_async_copy(src, dst, in_sem.at[i])
        for i, (src, dst) in enumerate(
            (
                (k_hbm, k_in), (v_hbm, v_in), (q_hbm, q_in), (h_hbm, h_in),
                (gain_hbm, gain_in), (taps_hbm, taps_in),
            )
        )
    ]
    for load in loads[:2]:
        load.start()
    barrier = pltpu.get_barrier_semaphore()

    def greet(device):
        pl.semaphore_signal(barrier, inc=1, device_id=device, device_id_type=pl.DeviceIdType.MESH)

    for step in range(1, peers):
        greet(place(others(step)))
    rounds = range((planes - 1).bit_length())

    def sender(l):
        return (plane + 1) % 2 ** (l + 1) == 2**l

    def receiver(l):
        return (plane // 2**l) % 2 == 1

    partners = ()
    for l in rounds:
        partners += tuple((sender(l) & (plane + 1 + k < planes), f + (1 + k) * group) for k in range(2**l))
        partners += ((receiver(l), (plane // 2**l * 2**l - 1) * group + inner),)
    if group > 1:
        partners += (((inner == 0) & (f > 0), f - 1), ((inner == group - 1) & (f < n_frame - 1), f + 1))
    for there, index in partners:
        pl.when(there)(functools.partial(greet, at_frame(index)))

    loads[2].start()
    w_loads = []
    w_first = [0]
    for s in range(slots):
        for p in owners(s):
            i = len(w_loads)
            w_loads.append(
                pltpu.make_async_copy(
                    w_hbm.at[pl.ds((first(p) + s) * dh, dh), :], w_in.at[i, pl.ds(0, dh), :], w_sem.at[i]
                )
            )
        w_first.append(len(w_loads))

    token_frame = lax.broadcasted_iota(jnp.int32, (tokens, 1), 0) // per_frame
    mask = token_frame < valid_ref[0]
    zeros = jnp.zeros((tokens, LANES - dh), bf16)
    ones = (lax.broadcasted_iota(jnp.int32, (tokens, LANES - dh), 1) == 0).astype(f32).astype(bf16)

    def put(dst, s, low, value, tail):
        for p in owners(s):
            h = first(p) + s
            dst[s, p, low : low + tokens] = jnp.concatenate([value[:, h * dh : (h + 1) * dh], tail], axis=1)

    def feature(ref):
        return jnp.where(mask, jnp.maximum(ref[...].astype(f32).reshape(tokens, feats), 0.0), 0.0).astype(bf16)

    class Exchange:
        def __init__(self, out, all_, send, recv):
            self.refs = out, all_, send, recv

        def copy(self, s, step):
            out, all_, send, recv = self.refs
            return pltpu.make_async_remote_copy(
                src_ref=out.at[s, others(step)],
                dst_ref=all_.at[s, me],
                send_sem=send.at[s, step],
                recv_sem=recv.at[s, step],
                device_id=place(others(step)),
                device_id_type=pl.DeviceIdType.MESH,
            )

        def start(self, s):
            out, all_, _, _ = self.refs
            for step in range(1, peers):
                where_owned(others(step), s, lambda step=step: self.copy(s, step).start())

            def keep():
                all_[s, pl.ds(me, 1)] = out[s, pl.ds(me, 1)]

            where_owned(me, s, keep)

        def arrived(self, s):
            for step in range(1, peers):
                self.copy(s, step).wait_recv()

        def sent(self, s):
            for step in range(1, peers):
                where_owned(others(step), s, lambda step=step: self.copy(s, step).wait_send())

    kv = Exchange(kv_out, kv_all, kv_send, kv_recv)
    query = Exchange(q_out, q_all, q_send, q_recv)

    loads[0].wait()
    key_feat = feature(k_in)
    loads[1].wait()
    value_feat = v_in[...].astype(f32).reshape(tokens, feats).astype(bf16)
    for s in range(slots):
        put(kv_out, s, 0, key_feat, zeros)
        put(kv_out, s, tokens, value_feat, ones)
        if s == 0:
            near = sum(there.astype(jnp.int32) for there, _ in partners)
            pl.semaphore_wait(barrier, peers - 1 + near)
        kv.start(s)
    loads[2].wait()
    query_feat = feature(q_in)
    for s in range(slots):
        put(q_out, s, 0, query_feat, zeros)
    def pass_on(s, l, k):
        return pltpu.make_async_remote_copy(
            src_ref=state_out.at[s],
            dst_ref=state_in.at[s, l],
            send_sem=s_send.at[s, k],
            recv_sem=s_recv.at[s, l],
            device_id=at_frame(f + (1 + k) * group),
            device_id_type=pl.DeviceIdType.MESH,
        )

    def each_target(s, l, act):
        for k in reversed(range(2**l)):
            pl.when(sender(l) & (plane + 1 + k < planes))(lambda k=k: act(pass_on(s, l, k)))

    def send_state(s, l, value):
        @pl.when(sender(l))
        def _():
            state_out[s] = value.astype(bf16)

        each_target(s, l, lambda copy: copy.start())

    def ranks(g):
        return slice(g * n_row, (g + 1) * n_row)

    def plane_state(s):
        kv.arrived(s)
        mine = []
        for g in range(group):
            keys = kv_all[s, ranks(g), 0:tokens].reshape(n_row * tokens, LANES)
            values = kv_all[s, ranks(g), tokens : 2 * tokens].reshape(n_row * tokens, LANES)
            mine.append(
                lax.dot_general(
                    keys, values, (((0,), (0,)), ((), ())), preferred_element_type=f32
                )[:dh]
            )
            state[s, g] = mine[-1]

        send_state(s, 0, sum(mine[1:], mine[0]))

    def chain(s):
        running = jnp.zeros((dh, LANES), f32)
        here = [state[s, g] for g in range(group)]
        for l in rounds:
            if l > 0:
                send_state(s, l, sum(here, running))

            @pl.when(receiver(l))
            def _():
                pass_on(s, l, 0).wait_recv()

            @pl.when(jnp.logical_not(receiver(l)))
            def _():
                state_in[s, l] = jnp.zeros((dh, LANES), bf16)

            running = running + state_in[s, l].astype(f32)
        for g in range(group):
            running = running + here[g]
            total[s, g] = running.astype(bf16)

    back = Exchange(att_out, att_all, a_send, a_recv)

    def attend(s):
        query.arrived(s)
        for g in range(group):
            queries = q_all[s, ranks(g)].reshape(n_row * tokens, LANES)[:, :dh]
            both = jnp.dot(queries, total[s, g], preferred_element_type=f32)
            value = both / (both[:, dh : dh + 1] + EPS_DEN)
            att_out[s, ranks(g)] = value.astype(bf16).reshape(n_row, tokens, LANES)

    def give_back(s):
        def mine():
            attend(s)
            for step in range(1, peers):
                back_copy(s, step).start()
            att_all[s, pl.ds(me, 1)] = att_out[s, pl.ds(me, 1)]

        where_owned(me, s, mine)

    def back_copy(s, step):
        return back.copy(s, step)

    relays = functools.reduce(jnp.logical_or, [sender(l) for l in rounds[1:]], plane < 0)

    def forward(s, when):
        pl.when(when)(lambda: where_owned(me, s, lambda: chain(s)))

    for s in range(slots):
        where_owned(me, s, lambda s=s: plane_state(s))
        if s == min(1, slots - 1):
            for later in range(slots):
                query.start(later)
            for load in w_loads + loads[3:]:
                load.start()
            w_in[:, dh:, :] = jnp.zeros((HEADS, LANES - dh, feats), bf16)
        if s > 0:
            forward(s - 1, relays)
    forward(slots - 1, relays)
    for s in range(slots):
        forward(s, jnp.logical_not(relays))
        give_back(s)

    loads[3].wait()
    half = -(-feats // (2 * LANES)) * LANES
    square = jnp.zeros((tokens, 1), f32)
    for s in range(slots):
        here = owners(s)
        for load in w_loads[w_first[s] : w_first[s + 1]]:
            load.wait()
        for step in range(1, peers):
            where_owned((me + peers - step) % peers, s, lambda step=step: back_copy(s, step).wait_recv())
        att = jnp.concatenate([att_all[s, p] for p in here], axis=1)
        depth = len(here) * LANES
        for low, high in ((0, half), (half, feats)):
            weights = w_in[w_first[s] : w_first[s + 1], :, low:high].reshape(depth, high - low)
            summed = jnp.dot(att, weights, preferred_element_type=f32)
            if s > 0:
                summed = res[:, low:high] + summed
            if s == slots - 1:
                hidden = h_in[:, :, :, low:high].astype(f32).reshape(tokens, high - low)
                summed = (hidden + summed).astype(bf16).astype(f32)
                square = square + jnp.sum(summed * summed, axis=1, keepdims=True)
            res[:, low:high] = summed
    inverse = lax.rsqrt(square / feats + EPS_NORM)
    loads[4].wait()
    gain = gain_in[...].reshape(1, feats)
    ext[tokens:, :] = (res[tokens - halo :, :] * inverse[tokens - halo :] * gain).astype(bf16)
    to_next = pltpu.make_async_remote_copy(
        src_ref=ext.at[pl.ds(tokens, halo), :],
        dst_ref=ext.at[pl.ds(0, halo), :],
        send_sem=halo_sem.at[0],
        recv_sem=halo_sem.at[1],
        device_id=at_frame(f + 1),
        device_id_type=pl.DeviceIdType.MESH,
    )
    pl.when(f < n_frame - 1)(lambda: to_next.start())
    if tokens > halo:
        ext[halo:tokens, :] = (res[: tokens - halo, :] * inverse[: tokens - halo] * gain).astype(bf16)

    @pl.when(f == 0)
    def _():
        ext[0:halo, :] = jnp.zeros((halo, feats), bf16)

    loads[5].wait()
    taps = taps_in[...]

    def mix(low, high):
        normed = ext[low : high + halo, :].astype(f32)
        temporal = jnp.zeros((high - low, feats), f32)
        for j in range(taps_n):
            start = (taps_n - 1 - j) * per_frame
            temporal = temporal + taps[j : j + 1] * normed[start : start + high - low]
        mixed = res[low:high, :] + temporal.astype(bf16).astype(f32)
        count = (high - low) // per_frame
        out_ref[low // per_frame : high // per_frame] = mixed.reshape(count, rows_dev, cols, feats).astype(bf16)

    if tokens > halo:
        mix(halo, tokens)
    for s in range(slots):
        kv.sent(s)
        query.sent(s)

        def gone(s=s):
            for step in range(1, peers):
                back_copy(s, step).wait_send()
            for l in rounds:
                each_target(s, l, lambda copy: copy.wait_send())

        where_owned(me, s, gone)
    pl.when(f > 0)(lambda: to_next.wait_recv())
    mix(0, min(halo, tokens))
    pl.when(f < n_frame - 1)(lambda: to_next.wait_send())


def body(n_frame, n_row, query_in, key_in, value_in, hidden_in, out_weight, norm_gain, temporal_taps, block_valid):
    frames, rows_dev, cols, feats = query_in.shape
    tokens = frames * rows_dev * cols
    group = 2 if n_frame % 2 == 0 else 1
    peers = group * n_row
    slots = -(-HEADS // peers)
    planes = n_frame // group
    rounds = max((planes - 1).bit_length(), 1)
    dh = feats // HEADS
    halo = (temporal_taps.shape[0] - 1) * rows_dev * cols
    bf16, f32 = jnp.bfloat16, jnp.float32
    hbm = pl.BlockSpec(memory_space=pltpu.HBM)
    vmem = pl.BlockSpec(memory_space=pltpu.VMEM)
    smem = pl.BlockSpec(memory_space=pltpu.SMEM)
    sems = pltpu.SemaphoreType.DMA
    return pl.pallas_call(
        functools.partial(kernel, n_frame, n_row, group, slots),
        out_shape=jax.ShapeDtypeStruct(query_in.shape, bf16),
        in_specs=[hbm] * 7 + [smem],
        out_specs=vmem,
        scratch_shapes=[
            pltpu.VMEM(query_in.shape, bf16),
            pltpu.VMEM(query_in.shape, bf16),
            pltpu.VMEM(query_in.shape, bf16),
            pltpu.VMEM(query_in.shape, bf16),
            pltpu.VMEM(norm_gain.shape, f32),
            pltpu.VMEM(temporal_taps.shape, f32),
            pltpu.VMEM((HEADS, LANES, feats), bf16),
            pltpu.VMEM((slots, peers, 2 * tokens, LANES), bf16),
            pltpu.VMEM((slots, peers, 2 * tokens, LANES), bf16),
            pltpu.VMEM((slots, peers, tokens, LANES), bf16),
            pltpu.VMEM((slots, peers, tokens, LANES), bf16),
            pltpu.VMEM((slots, group, dh, LANES), f32),
            pltpu.VMEM((slots, group, dh, LANES), bf16),
            pltpu.VMEM((slots, rounds, dh, LANES), bf16),
            pltpu.VMEM((slots, dh, LANES), bf16),
            pltpu.VMEM((slots, peers, tokens, LANES), bf16),
            pltpu.VMEM((slots, peers, tokens, LANES), bf16),
            pltpu.VMEM((tokens, feats), f32),
            pltpu.VMEM((tokens + halo, feats), bf16),
            sems((6,)),
            sems((HEADS,)),
            sems((slots, peers)),
            sems((slots, peers)),
            sems((slots, peers)),
            sems((slots, peers)),
            sems((slots, max(planes // 2, 1))),
            sems((slots, rounds)),
            sems((slots, peers)),
            sems((slots, peers)),
            sems((2,)),
        ],
        compiler_params=pltpu.CompilerParams(
            collective_id=0, has_side_effects=True, vmem_limit_bytes=63 * 1024 * 1024
        ),
        cost_estimate=pl.CostEstimate(
            flops=2 * tokens * feats * feats, bytes_accessed=2 * feats * feats, transcendentals=0
        ),
        name="block_forward",
    )(query_in, key_in, value_in, hidden_in, out_weight, norm_gain, temporal_taps, block_valid)


def solution(mesh):
    split = P("frame", "row", None, None)
    placed = (split, split, split, split, P(), P(), P(), P("frame"))
    n_frame, n_row = mesh.shape["frame"], mesh.shape["row"]
    return jax.shard_map(
        functools.partial(body, n_frame, n_row),
        mesh=mesh,
        in_specs=placed,
        out_specs=split,
        check_vma=False,
    )
```
